32 devices in a mesh: row: 8 (over z, y), col: 4 (over x, core).
Axes of the slice: x: 2, y: 2, z: 4, core: 2. Of those that a mesh axis runs over, the one named last changes fastest.
Arguments:
- inputs: bfloat16 [32, 256, 2048], P('row', 'col'), may hold values from -6 to 6
- output_gradient: bfloat16 [32, 256, 256], P('row', 'col'), may hold values from -6 to 6
- weight: bfloat16 [3, 3, 2048, 256], P(None, None, 'row'), may hold values from -0.125 to 0.125
Outputs:
- grad_in: bfloat16 [32, 256, 2048], P('row', 'col')
- grad_weight: float32 [3, 3, 2048, 256], P(None, None, 'row')
The draws below stay inside these ranges and needn't reach their ends.
All inputs are finite; a program needn't handle non-finite values.
Results may differ from the reference program's by a relative error of at most 0.001.
Values may be sent and summed in bfloat16 or wider, within the bound.
No kernel may reach another device: no remote copies, remote signals or barrier semaphores. Data moves between devices by JAX's collectives and lax.ppermute only.
A program may use at most 128 MiB of HBM per device.

```python
import math
import jax
import jax.numpy as jnp

CIN = 2048
COUT = 256
DILATION_STEP = 12
NH = 32
NW = 256


def raised(entries, own_key, source, target, shards_of, factor):
    def block_of(position):
        return (jnp.arange(entries.shape[position]) // (entries.shape[position] // shards_of)).reshape((-1,) + (1,) * (entries.ndim - 1 - position))

    near = jax.random.permutation(own_key, shards_of)[block_of(target)]
    second = (block_of(target) + shards_of // 2) % shards_of
    return jnp.where((block_of(source) == near) | (block_of(source) == second), factor * entries, entries)


def steps_of(rng, dims, shards, smallest, top_value):
    factor_of = 1.0
    for axis_at, blocks in shards:
        draws = jax.random.uniform(jax.random.fold_in(jax.random.fold_in(rng, 6), axis_at), (blocks,), jnp.float32, smallest / len(shards), top_value / len(shards))
        factor_of = factor_of * jnp.repeat(jnp.exp(draws), dims[axis_at] // blocks).reshape((-1,) + (1,) * (len(dims) - 1 - axis_at))
    return factor_of


def noise(stream_key, dims, deviation, reach, cuts=(), held_as=jnp.bfloat16):
    gain = steps_of(stream_key, dims, cuts, -0.22, 0.18) if cuts else 1.0
    result = jax.random.normal(stream_key, dims, jnp.float32) * deviation * gain
    return jnp.minimum(jnp.maximum(result, -reach), reach).astype(held_as)


def gaussian_with(own_key, dims, deviation, reach, cuts, heavy, kind=jnp.bfloat16):
    drawn = deviation * jax.random.normal(own_key, dims, jnp.float32)
    if cuts:
        drawn = drawn * steps_of(own_key, dims, cuts, -0.22, 0.18)
    return jnp.clip(raised(drawn, jax.random.fold_in(own_key, 3), *heavy), -reach, reach).astype(kind)


def setup_inputs(seed: int = 0) -> dict:
    keys = jax.random.split(jax.random.key(seed), 4)
    inputs = gaussian_with(keys[0], (NH, NW, CIN), 1.0, 6.0, ((0, 8), (1, 4)), (0, 2, 8, 2.0))
    output_gradient = gaussian_with(keys[1], (NH, NW, COUT), 1.0, 6.0, ((0, 8), (1, 4)), (1, 2, 4, 2.0))
    weight = noise(keys[2], (3, 3, CIN, COUT), (9 * COUT) ** -0.5, 0.125, ((2, 8),))
    return {"inputs": inputs, "output_gradient": output_gradient, "weight": weight}


def reference(inputs, output_gradient, weight):
    height, width, in_chans = inputs.shape
    out_chans = output_gradient.shape[2]
    padded_gradient = jnp.pad(output_gradient, ((DILATION_STEP, DILATION_STEP), (DILATION_STEP, DILATION_STEP), (0, 0)))
    flat_in = inputs.reshape(height * width, in_chans)
    grad_in = jnp.zeros((height * width, in_chans), jnp.float32)
    taps = []
    for kernel_tap_row in range(3):
        for kernel_tap_column in range(3):
            top_offset = DILATION_STEP * (2 - kernel_tap_row)
            left_offset = DILATION_STEP * (2 - kernel_tap_column)
            window = padded_gradient[top_offset:top_offset + height, left_offset:left_offset + width].reshape(height * width, out_chans)
            grad_in = grad_in + jnp.dot(window, weight[kernel_tap_row, kernel_tap_column].T, preferred_element_type=jnp.float32)
            taps.append(jnp.dot(flat_in.T, window, preferred_element_type=jnp.float32))
    scale = 1.0 / math.sqrt(height * width)
    grad_weight = jnp.stack(taps).reshape(3, 3, in_chans, out_chans) * scale
    return (grad_in.reshape(height, width, in_chans).astype(jnp.bfloat16), grad_weight)
```

```python
import math

import jax
import jax.numpy as jnp
from jax import lax
from jax.experimental import pallas as pl
from jax.experimental.pallas import tpu as pltpu
from jax.sharding import PartitionSpec as P

DILATION_STEP = 12
VMEM_LIMIT = 48 * 1024 * 1024


def swap(x, axis, bit):
    return lax.ppermute(x, axis, [(i, i ^ bit) for i in range(lax.axis_size(axis))])


def rims(x, width):
    peers, length = lax.axis_size("col"), x.shape[-2]
    up = [(i, i + 1) for i in range(peers - 1)]
    down = [(j, i) for i, j in up]
    before = lax.ppermute(x[..., length - width :, :], "col", up)
    after = lax.ppermute(x[..., :width, :], "col", down)
    return before, after


def back_kernel(me_ref, own_ref, z_refs, y_ref, left_ref, right_ref, weight_ref, back_ref, windows_ref):
    me = me_ref[0]
    tiles, positions, chans = back_ref.shape
    rows, step, outs = left_ref.shape[1:]
    width = positions // rows
    shift = DILATION_STEP // rows
    for k in range(tiles):
        if k % 2:
            tile = y_ref[k // 2]
        else:
            tile = z_refs[k // 2 - 1][...] if k else own_ref[...]
        tile = tile.astype(jnp.float32)
        left = left_ref[k].astype(jnp.float32)
        right = right_ref[k].astype(jnp.float32)
        shifted = (
            jnp.concatenate([tile[:, step:], right], axis=1),
            tile,
            jnp.concatenate([left, tile[:, : width - step]], axis=1),
        )
        for b in range(3):
            windows_ref[me ^ k, :, b * outs : (b + 1) * outs] = (
                shifted[b].reshape(positions, outs).astype(jnp.bfloat16)
            )
    for j in range(tiles):
        taps = [a for a in range(3) if 0 <= j - shift * (a - 1) < tiles]
        lhs = jnp.concatenate([windows_ref[j - shift * (a - 1)] for a in taps], axis=1)
        rhs = weight_ref[taps[0] * 3 * outs : (taps[-1] + 1) * 3 * outs, :]
        back_ref[j] = jnp.dot(lhs, rhs, preferred_element_type=jnp.float32).astype(back_ref.dtype)


def taps_kernel(rows, scale, core_ref, in_ref, windows_ref, mine_ref, other_ref, flipped_ref):
    core = core_ref[0]
    tiles, positions, chans = in_ref.shape
    half = chans // 2
    outs = windows_ref.shape[2] // 3
    shift = DILATION_STEP // rows
    for j in range(tiles):
        x = in_ref[j]
        low, high = x[:, :half], x[:, half:]
        mine = jnp.where(core == 0, low, high)
        other = jnp.where(core == 0, high, low)
        flipped_ref[:half, j * positions : (j + 1) * positions] = mine.T
        flipped_ref[half:, j * positions : (j + 1) * positions] = other.T
    for a in range(3):
        move = shift * (a - 1)
        first, last = max(0, move), min(tiles, tiles + move)
        lhs = flipped_ref[:, first * positions : last * positions]
        rhs = windows_ref[first - move : last - move].reshape((last - first) * positions, 3 * outs)
        terms = jnp.dot(lhs, rhs, preferred_element_type=jnp.float32) * scale
        for b in range(3):
            mine_ref[3 * a + b] = terms[:half, b * outs : (b + 1) * outs]
            other_ref[3 * a + b] = terms[half:, b * outs : (b + 1) * outs]


def vmem(n):
    return [pl.BlockSpec(memory_space=pltpu.VMEM)] * n


def quick(inputs, output_gradient, weight):
    rows, width, in_chans = inputs.shape
    outs = output_gradient.shape[2]
    tiles = lax.axis_size("row")
    panel = in_chans // tiles
    positions = rows * width
    me = lax.axis_index("row").astype(jnp.int32)
    core = (lax.axis_index("col") % 2).astype(jnp.int32)
    params = pltpu.CompilerParams(vmem_limit_bytes=VMEM_LIMIT)

    z_tiles = [swap(output_gradient, "row", k) for k in (2, 4, 6)]
    blocks = inputs.reshape(positions, tiles, panel).transpose(1, 0, 2)
    in_strip = lax.all_to_all(blocks, "row", split_axis=0, concat_axis=0, tiled=True)

    column = jnp.stack([output_gradient, *z_tiles])
    y_tiles = swap(column, "row", 1)
    both = jnp.stack([column, y_tiles], axis=1).reshape(tiles, rows, width, outs)
    left, right = rims(both, DILATION_STEP)
    flat_weight = weight.transpose(0, 1, 3, 2).reshape(9 * outs, panel)

    smem = pl.BlockSpec(memory_space=pltpu.SMEM)
    back, windows = pl.pallas_call(
        lambda me_ref, own, z1, z2, z3, y, lf, rt, w, back_ref, win_ref: back_kernel(
            me_ref, own, (z1, z2, z3), y, lf, rt, w, back_ref, win_ref
        ),
        out_shape=(
            jax.ShapeDtypeStruct((tiles, positions, panel), jnp.bfloat16),
            jax.ShapeDtypeStruct((tiles, positions, 3 * outs), jnp.bfloat16),
        ),
        in_specs=[smem] + vmem(8),
        out_specs=tuple(vmem(2)),
        compiler_params=params,
        name="back",
    )(me.reshape(1), output_gradient, *z_tiles, y_tiles, left, right, flat_weight)

    height = rows * tiles
    scale = 1.0 / math.sqrt(height * width * lax.axis_size("col"))
    half = jax.ShapeDtypeStruct((9, panel // 2, outs), jnp.float32)
    mine, other = pl.pallas_call(
        lambda *refs: taps_kernel(rows, scale, *refs),
        out_shape=(half, half),
        in_specs=[smem] + vmem(2),
        out_specs=tuple(vmem(2)),
        scratch_shapes=[pltpu.VMEM((panel, tiles * positions), jnp.bfloat16)],
        compiler_params=params,
        name="taps",
    )(core.reshape(1), in_strip, windows)

    grad_back = lax.all_to_all(back, "row", split_axis=0, concat_axis=0, tiled=True)
    grad_in = grad_back.transpose(1, 0, 2).reshape(rows, width, in_chans)

    chip = [mine[3 * a : 3 * a + 3] + swap(other[3 * a : 3 * a + 3], "col", 1) for a in range(3)]
    total = [c + swap(c, "col", 2) for c in chip]
    sibling = [swap(t, "col", 1) for t in total]
    grad_weight = jnp.stack(
        [
            jnp.where(core == 0, jnp.concatenate([t, s], axis=1), jnp.concatenate([s, t], axis=1))
            for t, s in zip(total, sibling)
        ]
    ).reshape(3, 3, panel, outs)
    return grad_in, grad_weight


def extended(x, sides, width):
    for axis, dim in sides:
        peers, length = (lax.axis_size(axis), x.shape[dim])
        up = [(i, (i + 1) % peers) for i in range(peers - 1)]
        down = [(j, i) for i, j in up]
        last = lax.slice_in_dim(x, length - width, length, axis=dim)
        initial = lax.slice_in_dim(x, 0, width, axis=dim)
        before = lax.ppermute(last, axis, up)
        after = lax.ppermute(initial, axis, down)
        x = jnp.concatenate([before, x, after], axis=dim)
    return x


def general(inputs, output_gradient, weight):
    height, width, in_chans = inputs.shape
    out_chans = output_gradient.shape[2]
    step = DILATION_STEP
    in_strip = lax.all_to_all(inputs, "row", split_axis=2, concat_axis=0, tiled=True)
    strip_rows = in_strip.shape[0]
    panel = in_strip.shape[2]
    in_padded = jnp.pad(in_strip, ((step, step), (0, 0), (0, 0)))
    side_rimmed = extended(output_gradient, (("col", 1),), step)
    piece = lax.all_gather(side_rimmed, "row", axis=0, tiled=True)
    start = jnp.int32(0)
    grad_padded = jnp.zeros((strip_rows + 2 * step, width, panel), jnp.float32)
    count = piece.shape[0]
    new_terms = []
    for kernel_tap_row in range(3):
        in_rows = lax.dynamic_slice_in_dim(in_padded, step * kernel_tap_row, count, 0).reshape(
            count * width, panel
        )
        back = jnp.zeros((count * width, panel), jnp.float32)
        for kernel_tap_column in range(3):
            left_offset = step * (2 - kernel_tap_column)
            window = piece[:, left_offset : left_offset + width, :].reshape(
                count * width, out_chans
            )
            new_terms.append(
                lax.dot_general(
                    in_rows, window, (((0,), (0,)), ((), ())), preferred_element_type=jnp.float32
                )
            )
            back = back + lax.dot_general(
                window,
                weight[kernel_tap_row, kernel_tap_column],
                (((1,), (1,)), ((), ())),
                preferred_element_type=jnp.float32,
            )
        target = start + step * kernel_tap_row
        current = lax.dynamic_slice_in_dim(grad_padded, target, count, 0)
        grad_padded = lax.dynamic_update_slice_in_dim(
            grad_padded, current + back.reshape(count, width, panel), target, 0
        )
    terms = jnp.stack(new_terms).reshape(3, 3, panel, out_chans)
    terms, grad_padded = (terms, grad_padded)
    grad_strip = grad_padded[step : step + strip_rows].astype(jnp.bfloat16)
    grad_in = lax.all_to_all(grad_strip, "row", split_axis=0, concat_axis=2, tiled=True)
    scale = 1.0 / math.sqrt(height * width * lax.axis_size("row") * lax.axis_size("col"))
    terms = terms * scale
    grad_weight = lax.psum(terms, "col")
    return (grad_in, grad_weight)


def shards(inputs, output_gradient, weight):
    rows, width, in_chans = inputs.shape
    tiles, strips = lax.axis_size("row"), lax.axis_size("col")
    fits = (
        tiles == 8
        and strips == 4
        and DILATION_STEP % rows == 0
        and DILATION_STEP <= width
        and width % 16 == 0
        and in_chans % (tiles * 256) == 0
        and output_gradient.shape[2] % 128 == 0
    )
    return (quick if fits else general)(inputs, output_gradient, weight)


def solution(mesh):
    return jax.shard_map(
        shards,
        mesh=mesh,
        in_specs=(P("row", "col", None), P("row", "col", None), P(None, None, "row", None)),
        out_specs=(P("row", "col", None), P(None, None, "row", None)),
        check_vma=False,
    )
```

```python
import math

import jax
import jax.numpy as jnp
from jax import lax
from jax.experimental import pallas as pl
from jax.experimental.pallas import tpu as pltpu
from jax.sharding import PartitionSpec as P

DILATION_STEP = 12
VMEM_LIMIT = 32 * 1024 * 1024


def swap(x, axis, bit):
    return lax.ppermute(x, axis, [(i, i ^ bit) for i in range(lax.axis_size(axis))])


def rims(x, width):
    peers, length = lax.axis_size("col"), x.shape[-2]
    up = [(i, i + 1) for i in range(peers - 1)]
    down = [(j, i) for i, j in up]
    before = lax.ppermute(x[..., length - width :, :], "col", up)
    after = lax.ppermute(x[..., :width, :], "col", down)
    return before, after


def split_kernel(y_ref, in_ref, own_ref, stay_ref, go_ref):
    zs, _, panel = stay_ref.shape
    for y in range(2):

        @pl.when(y_ref[0] == y)
        def _(y=y):
            for z in range(zs):
                for ref, keep in ((stay_ref, y), (go_ref, 1 - y)):
                    first = (2 * z + keep) * panel
                    ref[z] = in_ref[:, first : first + panel]

    go_ref[zs] = own_ref[...]


def pack_kernel(z_ref, stay_ref, got_ref, *out_refs):
    for k, out_ref in enumerate(out_refs):
        out_ref[0] = stay_ref[z_ref[0] ^ k]
        out_ref[1] = got_ref[z_ref[0] ^ k]


def merge_kernel(block_ref, out_ref):
    tiles, _, chans = block_ref.shape
    for t in range(tiles):
        out_ref[:, t * chans : (t + 1) * chans] = block_ref[t]


def windows_of(me_ref, own_ref, own_y_ref, rest_ref, rest_y_ref, left_ref, right_ref, windows_ref):
    me = me_ref[0]
    rows, step, outs = left_ref.shape[1:]
    count = left_ref.shape[0] // 2
    width = own_ref.shape[1]
    positions = rows * width
    pad = (windows_ref.shape[0] - 2 * count) // 2
    zeros = jnp.zeros(windows_ref.shape[1:], windows_ref.dtype)
    for k in range(pad):
        windows_ref[k] = zeros
        windows_ref[pad + 2 * count + k] = zeros
    for k in range(2 * count):
        z, other = k // 2, k % 2
        first, more = (own_y_ref, rest_y_ref) if other else (own_ref, rest_ref)
        tile = more[z - 1] if z else first[...]
        at = (count - 1) * other + z + 1 if z else other
        left, right = left_ref[at], right_ref[at]
        tile, left, right = (v.astype(jnp.float32) for v in (tile, left, right))
        shifted = (
            jnp.concatenate([tile[:, step:], right], axis=1),
            tile,
            jnp.concatenate([left, tile[:, : width - step]], axis=1),
        )
        for b in range(3):
            windows_ref[pad + (me ^ k), :, b * outs : (b + 1) * outs] = (
                shifted[b].reshape(positions, outs).astype(jnp.bfloat16)
            )


def back_kernel(shift, me_ref, *refs):
    *piece_refs, weight_ref, back_ref, windows_ref = refs
    windows_of(me_ref, *piece_refs, windows_ref)
    for j in range(back_ref.shape[0]):
        lhs = jnp.concatenate([windows_ref[j - shift * (a - 2)] for a in range(3)], axis=1)
        back_ref[j] = jnp.dot(
            lhs, weight_ref[...], preferred_element_type=jnp.float32
        ).astype(back_ref.dtype)


def taps_kernel(pad, scale, parts, me_ref, core_ref, *refs):
    in_refs, piece_refs, refs = refs[:parts], refs[parts:-3], refs[-3:]
    piece_refs, out_refs = piece_refs[:-4], piece_refs[-4:]
    windows_ref, strip_ref, flipped_ref = refs
    windows_of(me_ref, *piece_refs, windows_ref)
    core, me = core_ref[0], me_ref[0]
    tiles, positions, chans = strip_ref.shape
    half = chans // len(out_refs)
    outs = windows_ref.shape[2] // 3
    for k in range(tiles):
        strip_ref[me ^ k] = in_refs[k // 2][k % 2]
    for j in range(tiles):
        x = strip_ref[j]
        for c in range(len(out_refs) // 2):
            first = 2 * half * c
            low, high = x[:, first : first + half], x[:, first + half : first + 2 * half]
            mine = jnp.where(core == 0, low, high)
            other = jnp.where(core == 0, high, low)
            columns = slice(j * positions, (j + 1) * positions)
            flipped_ref[first : first + half, columns] = mine.T
            flipped_ref[first + half : first + 2 * half, columns] = other.T
    for a in range(3):
        move = pad * (a - 1)
        first, last = max(0, move), min(tiles, tiles + move)
        lhs = flipped_ref[:, first * positions : last * positions]
        rhs = windows_ref[pad + first - move : pad + last - move].reshape(
            (last - first) * positions, 3 * outs
        )
        terms = jnp.dot(lhs, rhs, preferred_element_type=jnp.float32) * scale
        for n, out_ref in enumerate(out_refs):
            for b in range(3):
                out_ref[3 * a + b] = terms[n * half : (n + 1) * half, b * outs : (b + 1) * outs]


def join_kernel(core_ref, *refs):
    *parts, out_ref = refs
    core = core_ref[0]
    half = parts[0].shape[1]
    for c in range(len(parts) // 4):
        mine, mine_x, other, other_x = parts[4 * c : 4 * c + 4]
        base = 2 * half * c
        out_ref[:, pl.ds(base + core * half, half), :] = mine[...] + mine_x[...]
        out_ref[:, pl.ds(base + (1 - core) * half, half), :] = other[...] + other_x[...]


def vmem(n):
    return [pl.BlockSpec(memory_space=pltpu.VMEM)] * n


def whole(*arrays):
    return [pl.BlockSpec(a.shape, lambda i, n=a.ndim: (0,) * n) for a in arrays]


CHUNKS = 2


def quick(inputs, output_gradient, weight):
    rows, width, in_chans = inputs.shape
    outs = output_gradient.shape[2]
    tiles = lax.axis_size("row")
    panel = in_chans // tiles
    chunk = panel // CHUNKS
    positions = rows * width
    shift = DILATION_STEP // rows
    me = lax.axis_index("row").astype(jnp.int32).reshape(1)
    core = (lax.axis_index("col") % 2).astype(jnp.int32).reshape(1)
    params = pltpu.CompilerParams(vmem_limit_bytes=VMEM_LIMIT)
    smem = pl.BlockSpec(memory_space=pltpu.SMEM)

    zs = tiles // 2
    flat = inputs.reshape(positions, in_chans)
    stay, go = pl.pallas_call(
        split_kernel,
        grid=(2,),
        out_shape=[
            jax.ShapeDtypeStruct((n, positions, panel), jnp.bfloat16) for n in (zs, zs + 1)
        ],
        in_specs=[
            smem,
            pl.BlockSpec((positions // 2, in_chans), lambda i: (i, 0)),
            pl.BlockSpec((positions // 2, outs), lambda i: (i, 0)),
        ],
        out_specs=[
            pl.BlockSpec((n, positions // 2, panel), lambda i: (0, i, 0)) for n in (zs, zs + 1)
        ],
        compiler_params=params,
        name="split",
    )(me % 2, flat, output_gradient.reshape(positions, outs))
    flat_weight = weight.transpose(0, 1, 3, 2).reshape(9 * outs, panel)
    rest = jnp.stack([swap(output_gradient, "row", k) for k in (2, 4, 6)])
    got = swap(go, "row", 1)
    got, flat_weight = lax.optimization_barrier((got, flat_weight))
    pairs = pl.pallas_call(
        pack_kernel,
        grid=(1,),
        out_shape=[jax.ShapeDtypeStruct((2, positions, panel), jnp.bfloat16)] * zs,
        in_specs=[smem] + whole(stay, got),
        out_specs=[pl.BlockSpec((2, positions, panel), lambda i: (0, 0, 0))] * zs,
        compiler_params=params,
        name="pack",
    )(me // 2, stay, got)
    rest, *pairs = lax.optimization_barrier((rest, *pairs))
    strip = [p if k == 0 else swap(p, "row", 2 * k) for k, p in enumerate(pairs)]

    rest_y = swap(rest, "row", 1)
    own_y = got[zs].reshape(rows, width, outs)
    stacked = jnp.concatenate([output_gradient[None], own_y[None], rest, rest_y])
    left, right = rims(stacked, DILATION_STEP)


    pieces = (output_gradient, own_y, rest, rest_y, left, right)
    windows = pltpu.VMEM((tiles + 2 * shift, positions, 3 * outs), jnp.bfloat16)

    back = pl.pallas_call(
        lambda *refs: back_kernel(shift, *refs),
        grid=(1,),
        out_shape=jax.ShapeDtypeStruct((tiles, positions, panel), jnp.bfloat16),
        in_specs=[smem] + whole(*pieces, flat_weight),
        out_specs=vmem(1)[0],
        scratch_shapes=[windows],
        compiler_params=params,
        name="back",
    )(me, *pieces, flat_weight)

    scale = 1.0 / math.sqrt(rows * tiles * width * lax.axis_size("col"))
    half = jax.ShapeDtypeStruct((9, chunk // 2, outs), jnp.float32)
    terms = pl.pallas_call(
        lambda *refs: taps_kernel(shift, scale, zs, *refs),
        grid=(1,),
        out_shape=(half,) * (2 * CHUNKS),
        in_specs=[smem, smem] + whole(*strip, *pieces),
        out_specs=tuple(vmem(2 * CHUNKS)),
        scratch_shapes=[
            windows,
            pltpu.VMEM((tiles, positions, panel), jnp.bfloat16),
            pltpu.VMEM((panel, tiles * positions), jnp.bfloat16),
        ],
        compiler_params=params,
        name="taps",
    )(me, core, *strip, *pieces)

    parts = []
    for mine, theirs in zip(terms[::2], terms[1::2]):
        chip = mine + swap(theirs, "col", 1)
        across = swap(chip, "col", 2)
        parts += [chip, across, swap(chip, "col", 1), swap(across, "col", 1)]

    grad_back = lax.all_to_all(back, "row", split_axis=0, concat_axis=0, tiled=True)
    grad_in = pl.pallas_call(
        merge_kernel,
        grid=(2,),
        out_shape=jax.ShapeDtypeStruct((positions, in_chans), jnp.bfloat16),
        in_specs=[pl.BlockSpec((tiles, positions // 2, panel), lambda i: (0, i, 0))],
        out_specs=pl.BlockSpec((positions // 2, in_chans), lambda i: (i, 0)),
        compiler_params=params,
        name="merge",
    )(grad_back)

    grad_weight = pl.pallas_call(
        join_kernel,
        grid=(3,),
        out_shape=jax.ShapeDtypeStruct((9, panel, outs), jnp.float32),
        in_specs=[smem] + [pl.BlockSpec((3, chunk // 2, outs), lambda i: (i, 0, 0))] * len(parts),
        out_specs=pl.BlockSpec((3, panel, outs), lambda i: (i, 0, 0)),
        compiler_params=params,
        name="join",
    )(core, *parts)
    return grad_in.reshape(rows, width, in_chans), grad_weight.reshape(3, 3, panel, outs)


def extended(x, sides, width):
    for axis, dim in sides:
        peers, length = (lax.axis_size(axis), x.shape[dim])
        up = [(i, (i + 1) % peers) for i in range(peers - 1)]
        down = [(j, i) for i, j in up]
        last = lax.slice_in_dim(x, length - width, length, axis=dim)
        initial = lax.slice_in_dim(x, 0, width, axis=dim)
        before = lax.ppermute(last, axis, up)
        after = lax.ppermute(initial, axis, down)
        x = jnp.concatenate([before, x, after], axis=dim)
    return x


def general(inputs, output_gradient, weight):
    height, width, in_chans = inputs.shape
    out_chans = output_gradient.shape[2]
    step = DILATION_STEP
    in_strip = lax.all_to_all(inputs, "row", split_axis=2, concat_axis=0, tiled=True)
    strip_rows = in_strip.shape[0]
    panel = in_strip.shape[2]
    in_padded = jnp.pad(in_strip, ((step, step), (0, 0), (0, 0)))
    side_rimmed = extended(output_gradient, (("col", 1),), step)
    piece = lax.all_gather(side_rimmed, "row", axis=0, tiled=True)
    start = jnp.int32(0)
    grad_padded = jnp.zeros((strip_rows + 2 * step, width, panel), jnp.float32)
    count = piece.shape[0]
    new_terms = []
    for kernel_tap_row in range(3):
        in_rows = lax.dynamic_slice_in_dim(in_padded, step * kernel_tap_row, count, 0).reshape(
            count * width, panel
        )
        back = jnp.zeros((count * width, panel), jnp.float32)
        for kernel_tap_column in range(3):
            left_offset = step * (2 - kernel_tap_column)
            window = piece[:, left_offset : left_offset + width, :].reshape(
                count * width, out_chans
            )
            new_terms.append(
                lax.dot_general(
                    in_rows, window, (((0,), (0,)), ((), ())), preferred_element_type=jnp.float32
                )
            )
            back = back + lax.dot_general(
                window,
                weight[kernel_tap_row, kernel_tap_column],
                (((1,), (1,)), ((), ())),
                preferred_element_type=jnp.float32,
            )
        target = start + step * kernel_tap_row
        current = lax.dynamic_slice_in_dim(grad_padded, target, count, 0)
        grad_padded = lax.dynamic_update_slice_in_dim(
            grad_padded, current + back.reshape(count, width, panel), target, 0
        )
    terms = jnp.stack(new_terms).reshape(3, 3, panel, out_chans)
    terms, grad_padded = (terms, grad_padded)
    grad_strip = grad_padded[step : step + strip_rows].astype(jnp.bfloat16)
    grad_in = lax.all_to_all(grad_strip, "row", split_axis=0, concat_axis=2, tiled=True)
    scale = 1.0 / math.sqrt(height * width * lax.axis_size("row") * lax.axis_size("col"))
    terms = terms * scale
    grad_weight = lax.psum(terms, "col")
    return (grad_in, grad_weight)


def shards(inputs, output_gradient, weight):
    rows, width, in_chans = inputs.shape
    tiles, strips = lax.axis_size("row"), lax.axis_size("col")
    fits = (
        tiles == 8
        and strips == 4
        and DILATION_STEP % rows == 0
        and DILATION_STEP <= width
        and width % 16 == 0
        and in_chans % (tiles * 256) == 0
        and output_gradient.shape[2] % 128 == 0
    )
    return (quick if fits else general)(inputs, output_gradient, weight)


def solution(mesh):
    return jax.shard_map(
        shards,
        mesh=mesh,
        in_specs=(P("row", "col", None), P("row", "col", None), P(None, None, "row", None)),
        out_specs=(P("row", "col", None), P(None, None, "row", None)),
        check_vma=False,
    )
```

```python
import math

import jax
import jax.numpy as jnp
from jax import lax
from jax.experimental import pallas as pl
from jax.experimental.pallas import tpu as pltpu
from jax.sharding import PartitionSpec as P

DILATION_STEP = 12
VMEM_LIMIT = 32 * 1024 * 1024


def swap(x, axis, bit):
    return lax.ppermute(x, axis, [(i, i ^ bit) for i in range(lax.axis_size(axis))])


def rims(x, width, core):
    peers, length = lax.axis_size("col"), x.shape[-2]
    first, last = x[..., :width, :], x[..., length - width :, :]
    near = swap(jnp.where(core == 0, last, first), "col", 1)
    pairs = [(i, i + 1) for i in range(1, peers - 1, 2)]
    beside = lax.ppermute(
        jnp.where(core == 0, first, last), "col", pairs + [(j, i) for i, j in pairs]
    )
    return near, beside


def split_kernel(me_ref, in_ref, own_ref, stay_ref, go_ref, go_far_ref):
    zs, _, panel = stay_ref.shape

    def channels(owner):
        return in_ref[:, pl.ds(pl.multiple_of(owner * panel, 128), panel)]

    for k in range(zs):
        owner = me_ref[0] ^ (2 * k)
        stay_ref[k] = channels(owner)
        if k < zs // 2:
            go_ref[k] = channels(owner ^ 1)
        else:
            go_far_ref[k - zs // 2] = channels(owner ^ 1)
    go_ref[zs // 2] = own_ref[...]


def pack_kernel(first, stay_ref, got_ref, *out_refs):
    for k, out_ref in enumerate(out_refs):
        out_ref[0] = stay_ref[first + k]
        out_ref[1] = got_ref[k]


def merge_kernel(block_ref, out_ref):
    tiles, _, chans = block_ref.shape
    for t in range(tiles):
        out_ref[:, t * chans : (t + 1) * chans] = block_ref[t]


def start_all(copies):
    for copy in copies:
        copy.start()
    return copies


def wait_all(copies):
    for copy in copies:
        copy.wait()


def piece_copies(piece_refs, tile_ref, near_ref, beside_ref, sem):
    own_ref, got_ref, rest_ref, rest_y_ref, near_from, beside_from = piece_refs
    tiles = tile_ref.shape[0]
    copies = []
    for k in range(tiles):
        if k < 2:
            source = got_ref.at[got_ref.shape[0] - 1] if k else own_ref
        else:
            source = (rest_y_ref if k % 2 else rest_ref).at[k // 2 - 1]
        copies.append(pltpu.make_async_copy(source, tile_ref.at[k], sem.at[k]))
    copies.append(pltpu.make_async_copy(near_from, near_ref, sem.at[tiles]))
    copies.append(pltpu.make_async_copy(beside_from, beside_ref, sem.at[tiles + 1]))
    return copies


def windows_of(me, core, tile_ref, near_ref, beside_ref, windows_ref):
    tiles, positions, outs = tile_ref.shape
    rows, step = near_ref.shape[1:3]
    width = positions // rows
    pad = (windows_ref.shape[0] - tiles) // 2
    zeros = jnp.zeros(windows_ref.shape[1:], windows_ref.dtype)
    for k in range(pad):
        windows_ref[k] = zeros
        windows_ref[pad + tiles + k] = zeros
    for k in range(tiles):
        tile = tile_ref[k].reshape(rows, width, outs)
        at = k if k < 2 else k // 2 + 1 + k % 2 * (tiles // 2 - 1)
        tile, near, beside = (
            v.astype(jnp.float32) for v in (tile, near_ref[at], beside_ref[at])
        )
        left = jnp.where(core == 0, beside, near)
        right = jnp.where(core == 0, near, beside)
        shifted = (
            jnp.concatenate([tile[:, step:], right], axis=1),
            tile,
            jnp.concatenate([left, tile[:, : width - step]], axis=1),
        )
        for b in range(3):
            windows_ref[pad + (me ^ k), :, b * outs : (b + 1) * outs] = (
                shifted[b].reshape(positions, outs).astype(jnp.bfloat16)
            )


def back_kernel(shift, me_ref, core_ref, *refs):
    piece_refs, weight_ref, back_ref = refs[:6], refs[6], refs[7]
    tile_ref, near_ref, beside_ref, windows_ref, sem = refs[8:]
    tiles = tile_ref.shape[0]
    copies = start_all(piece_copies(piece_refs, tile_ref, near_ref, beside_ref, sem))
    wait_all(copies)
    windows_of(me_ref[0], core_ref[0], tile_ref, near_ref, beside_ref, windows_ref)
    for j in range(tiles):
        lhs = jnp.concatenate([windows_ref[j - shift * (a - 2)] for a in range(3)], axis=1)
        back_ref[j] = jnp.dot(
            lhs, weight_ref[...], preferred_element_type=jnp.float32
        ).astype(back_ref.dtype)


def taps_kernel(pad, scale, count, me_ref, core_ref, *refs):
    piece_refs, strip_from, out_refs = refs[:6], refs[6 : 6 + count], refs[6 + count : -7]
    tile_ref, near_ref, beside_ref, windows_ref, strip_ref, flipped_ref, sem = refs[-7:]
    tiles, positions, chans = strip_ref.shape
    half = chans // len(out_refs)
    outs = tile_ref.shape[2]
    core, me = core_ref[0], me_ref[0]
    copies = start_all(piece_copies(piece_refs, tile_ref, near_ref, beside_ref, sem))
    strips = start_all(
        [
            pltpu.make_async_copy(
                ref, strip_ref.at[pl.ds(2 * k, 2)], sem.at[tiles + 2 + k]
            )
            for k, ref in enumerate(strip_from)
        ]
    )
    wait_all(copies)
    windows_of(me, core, tile_ref, near_ref, beside_ref, windows_ref)
    wait_all(strips)
    for j in range(tiles):
        x = strip_ref[me ^ j]
        for c in range(len(out_refs) // 2):
            first = 2 * half * c
            low, high = x[:, first : first + half], x[:, first + half : first + 2 * half]
            mine = jnp.where(core == 0, low, high)
            other = jnp.where(core == 0, high, low)
            columns = slice(j * positions, (j + 1) * positions)
            flipped_ref[first : first + half, columns] = mine.T
            flipped_ref[first + half : first + 2 * half, columns] = other.T
    for a in range(3):
        move = pad * (a - 1)
        first, last = max(0, move), min(tiles, tiles + move)
        lhs = flipped_ref[:, first * positions : last * positions]
        rhs = windows_ref[pad + first - move : pad + last - move].reshape(
            (last - first) * positions, 3 * outs
        )
        terms = jnp.dot(lhs, rhs, preferred_element_type=jnp.float32) * scale
        for n, out_ref in enumerate(out_refs):
            for b in range(3):
                out_ref[3 * a + b] = terms[n * half : (n + 1) * half, b * outs : (b + 1) * outs]


def join_kernel(core_ref, *refs):
    *parts, out_ref = refs
    core = core_ref[0]
    half = parts[0].shape[1]
    for c in range(len(parts) // 4):
        mine, mine_x, other, other_x = parts[4 * c : 4 * c + 4]
        base = 2 * half * c
        out_ref[:, pl.ds(base + core * half, half), :] = mine[...] + mine_x[...]
        out_ref[:, pl.ds(base + (1 - core) * half, half), :] = other[...] + other_x[...]


def vmem(n):
    return [pl.BlockSpec(memory_space=pltpu.VMEM)] * n


def whole(*arrays):
    return [pl.BlockSpec(a.shape, lambda i, n=a.ndim: (0,) * n) for a in arrays]


CHUNKS = 1


def quick(inputs, output_gradient, weight):
    rows, width, in_chans = inputs.shape
    outs = output_gradient.shape[2]
    tiles = lax.axis_size("row")
    panel = in_chans // tiles
    chunk = panel // CHUNKS
    positions = rows * width
    shift = DILATION_STEP // rows
    me = lax.axis_index("row").astype(jnp.int32).reshape(1)
    core = (lax.axis_index("col") % 2).astype(jnp.int32).reshape(1)
    params = pltpu.CompilerParams(vmem_limit_bytes=VMEM_LIMIT)
    smem = pl.BlockSpec(memory_space=pltpu.SMEM)

    zs = tiles // 2
    flat = inputs.reshape(positions, in_chans)
    sizes = (zs, zs // 2 + 1, zs // 2)
    stay, go, go_far = pl.pallas_call(
        split_kernel,
        grid=(2,),
        out_shape=[jax.ShapeDtypeStruct((n, positions, panel), jnp.bfloat16) for n in sizes],
        in_specs=[
            smem,
            pl.BlockSpec((positions // 2, in_chans), lambda i: (i, 0)),
            pl.BlockSpec((positions // 2, outs), lambda i: (i, 0)),
        ],
        out_specs=[pl.BlockSpec((n, positions // 2, panel), lambda i: (0, i, 0)) for n in sizes],
        compiler_params=params,
        name="split",
    )(me, flat, output_gradient.reshape(positions, outs))
    flat_weight = weight.transpose(0, 1, 3, 2).reshape(9 * outs, panel)
    own = output_gradient.reshape(positions, outs)
    rest = jnp.stack([swap(own, "row", k) for k in (2, 4, 6)])
    got_far = swap(go_far, "row", 1)
    got = swap(go, "row", 1)
    got, flat_weight = lax.optimization_barrier((got, flat_weight))

    def pack(first, arrived):
        count = zs // 2
        return pl.pallas_call(
            lambda *refs: pack_kernel(first, *refs),
            grid=(1,),
            out_shape=[jax.ShapeDtypeStruct((2, positions, panel), jnp.bfloat16)] * count,
            in_specs=whole(stay, arrived),
            out_specs=[pl.BlockSpec((2, positions, panel), lambda i: (0, 0, 0))] * count,
            compiler_params=params,
            name="pack",
        )(stay, arrived)

    far_pairs = pack(zs // 2, got_far)
    rest, *far_pairs = lax.optimization_barrier((rest, *far_pairs))
    pairs = [*pack(0, got), *far_pairs]
    strip = [p if k == 0 else swap(p, "row", 2 * k) for k, p in enumerate(pairs)]

    rest_y = swap(rest, "row", 1)
    stacked = jnp.concatenate([own[None], got[zs // 2 :], rest, rest_y])
    near, beside = rims(stacked.reshape(tiles, rows, width, outs), DILATION_STEP, core)

    pieces = (own, got, rest, rest_y, near, beside)
    hbm = pl.BlockSpec(memory_space=pltpu.HBM)
    buffers = [
        pltpu.VMEM((tiles, positions, outs), jnp.bfloat16),
        pltpu.VMEM(near.shape, jnp.bfloat16),
        pltpu.VMEM(beside.shape, jnp.bfloat16),
        pltpu.VMEM((tiles + 2 * shift, positions, 3 * outs), jnp.bfloat16),
    ]
    back = pl.pallas_call(
        lambda *refs: back_kernel(shift, *refs),
        out_shape=jax.ShapeDtypeStruct((tiles, positions, panel), jnp.bfloat16),
        in_specs=[smem, smem] + [hbm] * 6 + vmem(1),
        out_specs=vmem(1)[0],
        scratch_shapes=buffers + [pltpu.SemaphoreType.DMA((tiles + 2,))],
        compiler_params=params,
        name="back",
    )(me, core, *pieces, flat_weight)

    back, core = lax.optimization_barrier((back, core))
    scale = 1.0 / math.sqrt(rows * tiles * width * lax.axis_size("col"))
    half = jax.ShapeDtypeStruct((9, chunk // 2, outs), jnp.float32)
    terms = pl.pallas_call(
        lambda *refs: taps_kernel(shift, scale, zs, *refs),
        out_shape=(half,) * (2 * CHUNKS),
        in_specs=[smem, smem] + [hbm] * (6 + zs),
        out_specs=tuple(vmem(2 * CHUNKS)),
        scratch_shapes=buffers
        + [
            pltpu.VMEM((tiles, positions, panel), jnp.bfloat16),
            pltpu.VMEM((panel, tiles * positions), jnp.bfloat16),
            pltpu.SemaphoreType.DMA((tiles + 2 + zs,)),
        ],
        compiler_params=params,
        name="taps",
    )(me, core, *pieces, *strip)
    parts = []
    for mine, theirs in zip(terms[::2], terms[1::2]):
        chip = mine + swap(theirs, "col", 1)
        across = swap(chip, "col", 2)
        parts += [chip, across, swap(chip, "col", 1), swap(across, "col", 1)]

    grad_back = lax.all_to_all(back, "row", split_axis=0, concat_axis=0, tiled=True)
    grad_weight = pl.pallas_call(
        join_kernel,
        grid=(3,),
        out_shape=jax.ShapeDtypeStruct((9, panel, outs), jnp.float32),
        in_specs=[smem] + [pl.BlockSpec((3, chunk // 2, outs), lambda i: (i, 0, 0))] * len(parts),
        out_specs=pl.BlockSpec((3, panel, outs), lambda i: (i, 0, 0)),
        compiler_params=params,
        name="join",
    )(core, *parts)
    grad_back, grad_weight = lax.optimization_barrier((grad_back, grad_weight))
    grad_in = pl.pallas_call(
        merge_kernel,
        grid=(2,),
        out_shape=jax.ShapeDtypeStruct((positions, in_chans), jnp.bfloat16),
        in_specs=[pl.BlockSpec((tiles, positions // 2, panel), lambda i: (0, i, 0))],
        out_specs=pl.BlockSpec((positions // 2, in_chans), lambda i: (i, 0)),
        compiler_params=params,
        name="merge",
    )(grad_back)

    return grad_in.reshape(rows, width, in_chans), grad_weight.reshape(3, 3, panel, outs)


def extended(x, sides, width):
    for axis, dim in sides:
        peers, length = (lax.axis_size(axis), x.shape[dim])
        up = [(i, (i + 1) % peers) for i in range(peers - 1)]
        down = [(j, i) for i, j in up]
        last = lax.slice_in_dim(x, length - width, length, axis=dim)
        initial = lax.slice_in_dim(x, 0, width, axis=dim)
        before = lax.ppermute(last, axis, up)
        after = lax.ppermute(initial, axis, down)
        x = jnp.concatenate([before, x, after], axis=dim)
    return x


def general(inputs, output_gradient, weight):
    height, width, in_chans = inputs.shape
    out_chans = output_gradient.shape[2]
    step = DILATION_STEP
    in_strip = lax.all_to_all(inputs, "row", split_axis=2, concat_axis=0, tiled=True)
    strip_rows = in_strip.shape[0]
    panel = in_strip.shape[2]
    in_padded = jnp.pad(in_strip, ((step, step), (0, 0), (0, 0)))
    side_rimmed = extended(output_gradient, (("col", 1),), step)
    piece = lax.all_gather(side_rimmed, "row", axis=0, tiled=True)
    start = jnp.int32(0)
    grad_padded = jnp.zeros((strip_rows + 2 * step, width, panel), jnp.float32)
    count = piece.shape[0]
    new_terms = []
    for kernel_tap_row in range(3):
        in_rows = lax.dynamic_slice_in_dim(in_padded, step * kernel_tap_row, count, 0).reshape(
            count * width, panel
        )
        back = jnp.zeros((count * width, panel), jnp.float32)
        for kernel_tap_column in range(3):
            left_offset = step * (2 - kernel_tap_column)
            window = piece[:, left_offset : left_offset + width, :].reshape(
                count * width, out_chans
            )
            new_terms.append(
                lax.dot_general(
                    in_rows, window, (((0,), (0,)), ((), ())), preferred_element_type=jnp.float32
                )
            )
            back = back + lax.dot_general(
                window,
                weight[kernel_tap_row, kernel_tap_column],
                (((1,), (1,)), ((), ())),
                preferred_element_type=jnp.float32,
            )
        target = start + step * kernel_tap_row
        current = lax.dynamic_slice_in_dim(grad_padded, target, count, 0)
        grad_padded = lax.dynamic_update_slice_in_dim(
            grad_padded, current + back.reshape(count, width, panel), target, 0
        )
    terms = jnp.stack(new_terms).reshape(3, 3, panel, out_chans)
    terms, grad_padded = (terms, grad_padded)
    grad_strip = grad_padded[step : step + strip_rows].astype(jnp.bfloat16)
    grad_in = lax.all_to_all(grad_strip, "row", split_axis=0, concat_axis=2, tiled=True)
    scale = 1.0 / math.sqrt(height * width * lax.axis_size("row") * lax.axis_size("col"))
    terms = terms * scale
    grad_weight = lax.psum(terms, "col")
    return (grad_in, grad_weight)


def shards(inputs, output_gradient, weight):
    rows, width, in_chans = inputs.shape
    tiles, strips = lax.axis_size("row"), lax.axis_size("col")
    fits = (
        tiles == 8
        and strips == 4
        and DILATION_STEP % rows == 0
        and DILATION_STEP <= width
        and width % 16 == 0
        and in_chans % (tiles * 256) == 0
        and output_gradient.shape[2] % 128 == 0
    )
    return (quick if fits else general)(inputs, output_gradient, weight)


def solution(mesh):
    return jax.shard_map(
        shards,
        mesh=mesh,
        in_specs=(P("row", "col", None), P("row", "col", None), P(None, None, "row", None)),
        out_specs=(P("row", "col", None), P(None, None, "row", None)),
        check_vma=False,
    )
```

```python
import math

import jax
import jax.numpy as jnp
from jax import lax
from jax.experimental import pallas as pl
from jax.experimental.pallas import tpu as pltpu
from jax.sharding import PartitionSpec as P

DILATION_STEP = 12
VMEM_LIMIT = 32 * 1024 * 1024


def swap(x, axis, bit):
    return lax.ppermute(x, axis, [(i, i ^ bit) for i in range(lax.axis_size(axis))])


def rims(x, width, core):
    peers, length = lax.axis_size("col"), x.shape[-2]
    first, last = x[..., :width, :], x[..., length - width :, :]
    near = swap(jnp.where(core == 0, last, first), "col", 1)
    pairs = [(i, i + 1) for i in range(1, peers - 1, 2)]
    beside = lax.ppermute(
        jnp.where(core == 0, first, last), "col", pairs + [(j, i) for i, j in pairs]
    )
    return near, beside


def split_kernel(me_ref, in_ref, own_ref, stay_ref, go_ref, go_far_ref):
    zs, _, panel = stay_ref.shape

    def channels(owner):
        return in_ref[:, pl.ds(pl.multiple_of(owner * panel, 128), panel)]

    for k in range(zs):
        owner = me_ref[0] ^ (2 * k)
        stay_ref[k] = channels(owner)
        if k < zs // 2:
            go_ref[k] = channels(owner ^ 1)
        else:
            go_far_ref[k - zs // 2] = channels(owner ^ 1)
    go_ref[zs // 2] = own_ref[...]


def pack_kernel(first, stay_ref, got_ref, *out_refs):
    for k, out_ref in enumerate(out_refs):
        out_ref[0] = stay_ref[first + k]
        out_ref[1] = got_ref[k]


def merge_kernel(block_ref, out_ref):
    tiles, _, chans = block_ref.shape
    for t in range(tiles):
        out_ref[:, t * chans : (t + 1) * chans] = block_ref[t]


def start_all(copies):
    for copy in copies:
        copy.start()
    return copies


def wait_all(copies):
    for copy in copies:
        copy.wait()


def piece_copies(piece_refs, tile_ref, near_ref, beside_ref, sem):
    own_ref, got_ref, rest_ref, rest_y_ref, near_from, beside_from = piece_refs
    tiles = tile_ref.shape[0]
    copies = []
    for k in range(tiles):
        if k < 2:
            source = got_ref.at[got_ref.shape[0] - 1] if k else own_ref
        else:
            source = (rest_y_ref if k % 2 else rest_ref).at[k // 2 - 1]
        copies.append(pltpu.make_async_copy(source, tile_ref.at[k], sem.at[k]))
    copies.append(pltpu.make_async_copy(near_from, near_ref, sem.at[tiles]))
    copies.append(pltpu.make_async_copy(beside_from, beside_ref, sem.at[tiles + 1]))
    return copies


def windows_of(me, core, tile_ref, near_ref, beside_ref, windows_ref):
    tiles, positions, outs = tile_ref.shape
    rows, step = near_ref.shape[1:3]
    width = positions // rows
    pad = (windows_ref.shape[0] - tiles) // 2
    zeros = jnp.zeros(windows_ref.shape[1:], windows_ref.dtype)
    for k in range(pad):
        windows_ref[k] = zeros
        windows_ref[pad + tiles + k] = zeros
    for k in range(tiles):
        tile = tile_ref[k].reshape(rows, width, outs)
        at = k if k < 2 else k // 2 + 1 + k % 2 * (tiles // 2 - 1)
        tile, near, beside = (
            v.astype(jnp.float32) for v in (tile, near_ref[at], beside_ref[at])
        )
        left = jnp.where(core == 0, beside, near)
        right = jnp.where(core == 0, near, beside)
        shifted = (
            jnp.concatenate([tile[:, step:], right], axis=1),
            tile,
            jnp.concatenate([left, tile[:, : width - step]], axis=1),
        )
        for b in range(3):
            windows_ref[pad + (me ^ k), :, b * outs : (b + 1) * outs] = (
                shifted[b].reshape(positions, outs).astype(jnp.bfloat16)
            )


def windows_kernel(me_ref, core_ref, *refs):
    piece_refs, windows_ref = refs[:6], refs[6]
    tile_ref, near_ref, beside_ref, sem = refs[7:]
    wait_all(start_all(piece_copies(piece_refs, tile_ref, near_ref, beside_ref, sem)))
    windows_of(me_ref[0], core_ref[0], tile_ref, near_ref, beside_ref, windows_ref)


def back_kernel(shift, windows_ref, weight_ref, back_ref, flat_ref):
    tiles, depth = back_ref.shape[0], windows_ref.shape[2]
    outs = weight_ref.shape[2]
    for t in range(weight_ref.shape[0]):
        flat_ref[:, t * outs : (t + 1) * outs] = weight_ref[t]
    for j in range(tiles):
        taps = [a for a in range(3) if 0 <= j - shift * (a - 1) < tiles]
        lhs = jnp.concatenate([windows_ref[j - shift * (a - 2)] for a in taps], axis=1)
        rhs = flat_ref[:, taps[0] * depth : (taps[-1] + 1) * depth]
        back_ref[j] = lax.dot_general(
            lhs, rhs, (((1,), (1,)), ((), ())), preferred_element_type=jnp.float32
        ).astype(back_ref.dtype)


def terms_of(pad, scale, flipped, windows_ref, out_ref):
    positions, outs = windows_ref.shape[1], out_ref.shape[2]
    tiles = flipped.shape[1] // positions
    for a in range(3):
        move = pad * (a - 1)
        first, last = max(0, move), min(tiles, tiles + move)
        lhs = flipped[:, first * positions : last * positions]
        rhs = windows_ref[pad + first - move : pad + last - move].reshape(
            (last - first) * positions, 3 * outs
        )
        terms = jnp.dot(lhs, rhs, preferred_element_type=jnp.float32) * scale
        for b in range(3):
            out_ref[3 * a + b] = terms[:, b * outs : (b + 1) * outs]


def other_kernel(pad, scale, me_ref, core_ref, *refs):
    *strip_from, windows_ref, other_ref, mine_ref, strip_ref, flipped_ref, sem = refs
    tiles, positions, chans = strip_ref.shape
    half = chans // 2
    core, me = core_ref[0], me_ref[0]
    wait_all(
        start_all(
            [
                pltpu.make_async_copy(ref, strip_ref.at[pl.ds(2 * k, 2)], sem.at[k])
                for k, ref in enumerate(strip_from)
            ]
        )
    )
    for j in range(tiles):
        x = strip_ref[me ^ j]
        low, high = x[:, :half], x[:, half:]
        columns = slice(j * positions, (j + 1) * positions)
        mine_ref[:, columns] = jnp.where(core == 0, low, high).T
        flipped_ref[:, columns] = jnp.where(core == 0, high, low).T
    terms_of(pad, scale, flipped_ref, windows_ref, other_ref)


def mine_kernel(pad, scale, flipped_ref, windows_ref, mine_ref):
    terms_of(pad, scale, flipped_ref, windows_ref, mine_ref)


def join_kernel(half_ref, part_ref, part_x_ref, *refs):
    refs[-1][...] = part_ref[...] + part_x_ref[...]


def vmem(n):
    return [pl.BlockSpec(memory_space=pltpu.VMEM)] * n


def whole(*arrays):
    return [pl.BlockSpec(a.shape, lambda i, n=a.ndim: (0,) * n) for a in arrays]


def quick(inputs, output_gradient, weight):
    rows, width, in_chans = inputs.shape
    outs = output_gradient.shape[2]
    tiles = lax.axis_size("row")
    panel = in_chans // tiles
    positions = rows * width
    shift = DILATION_STEP // rows
    me = lax.axis_index("row").astype(jnp.int32).reshape(1)
    core = (lax.axis_index("col") % 2).astype(jnp.int32).reshape(1)
    params = pltpu.CompilerParams(vmem_limit_bytes=VMEM_LIMIT)
    smem = pl.BlockSpec(memory_space=pltpu.SMEM)

    zs = tiles // 2
    flat = inputs.reshape(positions, in_chans)
    sizes = (zs, zs // 2 + 1, zs // 2)
    stay, go, go_far = pl.pallas_call(
        split_kernel,
        grid=(2,),
        out_shape=[jax.ShapeDtypeStruct((n, positions, panel), jnp.bfloat16) for n in sizes],
        in_specs=[
            smem,
            pl.BlockSpec((positions // 2, in_chans), lambda i: (i, 0)),
            pl.BlockSpec((positions // 2, outs), lambda i: (i, 0)),
        ],
        out_specs=[pl.BlockSpec((n, positions // 2, panel), lambda i: (0, i, 0)) for n in sizes],
        compiler_params=params,
        name="split",
    )(me, flat, output_gradient.reshape(positions, outs))
    own = output_gradient.reshape(positions, outs)
    rest = jnp.stack([swap(own, "row", k) for k in (2, 4, 6)])
    got_far = swap(go_far, "row", 1)
    got = swap(go, "row", 1)

    def pack(first, arrived):
        count = zs // 2
        return pl.pallas_call(
            lambda *refs: pack_kernel(first, *refs),
            grid=(1,),
            out_shape=[jax.ShapeDtypeStruct((2, positions, panel), jnp.bfloat16)] * count,
            in_specs=whole(stay, arrived),
            out_specs=[pl.BlockSpec((2, positions, panel), lambda i: (0, 0, 0))] * count,
            compiler_params=params,
            name="pack",
        )(stay, arrived)

    far_pairs = pack(zs // 2, got_far)
    rest, *far_pairs = lax.optimization_barrier((rest, *far_pairs))
    pairs = [*pack(0, got), *far_pairs]
    strip = [p if k == 0 else swap(p, "row", 2 * k) for k, p in enumerate(pairs)]

    rest_y = swap(rest, "row", 1)
    stacked = jnp.concatenate([own[None], got[zs // 2 :], rest, rest_y])
    near, beside = rims(stacked.reshape(tiles, rows, width, outs), DILATION_STEP, core)

    pieces = (own, got, rest, rest_y, near, beside)
    hbm = pl.BlockSpec(memory_space=pltpu.HBM)
    windows = pl.pallas_call(
        windows_kernel,
        out_shape=jax.ShapeDtypeStruct((tiles + 2 * shift, positions, 3 * outs), jnp.bfloat16),
        in_specs=[smem, smem] + [hbm] * 6,
        out_specs=vmem(1)[0],
        scratch_shapes=[
            pltpu.VMEM((tiles, positions, outs), jnp.bfloat16),
            pltpu.VMEM(near.shape, jnp.bfloat16),
            pltpu.VMEM(beside.shape, jnp.bfloat16),
            pltpu.SemaphoreType.DMA((tiles + 2,)),
        ],
        compiler_params=params,
        name="windows",
    )(me, core, *pieces)
    back = pl.pallas_call(
        lambda *refs: back_kernel(shift, *refs),
        out_shape=jax.ShapeDtypeStruct((tiles, positions, panel), jnp.bfloat16),
        in_specs=vmem(2),
        out_specs=vmem(1)[0],
        scratch_shapes=[pltpu.VMEM((panel, 9 * outs), jnp.bfloat16)],
        compiler_params=params,
        name="back",
    )(windows, weight.reshape(9, panel, outs))
    back, core = lax.optimization_barrier((back, core))

    scale = 1.0 / math.sqrt(rows * tiles * width * lax.axis_size("col"))
    half = jax.ShapeDtypeStruct((9, panel // 2, outs), jnp.float32)
    theirs, flipped = pl.pallas_call(
        lambda *refs: other_kernel(shift, scale, *refs),
        out_shape=(half, jax.ShapeDtypeStruct((panel // 2, tiles * positions), jnp.bfloat16)),
        in_specs=[smem, smem] + [hbm] * zs + vmem(1),
        out_specs=tuple(vmem(2)),
        scratch_shapes=[
            pltpu.VMEM((tiles, positions, panel), jnp.bfloat16),
            pltpu.VMEM((panel // 2, tiles * positions), jnp.bfloat16),
            pltpu.SemaphoreType.DMA((zs,)),
        ],
        compiler_params=params,
        name="other_terms",
    )(me, core, *strip, windows)
    mine = pl.pallas_call(
        lambda *refs: mine_kernel(shift, scale, *refs),
        out_shape=half,
        in_specs=vmem(2),
        out_specs=vmem(1)[0],
        compiler_params=params,
        name="mine_terms",
    )(flipped, windows)
    chip = mine + swap(theirs, "col", 1)
    across = swap(chip, "col", 2)
    other = (swap(chip, "col", 1), swap(across, "col", 1))
    grad_weight = None
    for which, terms in ((core, (chip, across)), (1 - core, other)):
        before = [] if grad_weight is None else [grad_weight]
        block = (3, panel // 2, outs)
        grad_weight = pl.pallas_call(
            join_kernel,
            grid_spec=pltpu.PrefetchScalarGridSpec(
                num_scalar_prefetch=1,
                grid=(3,),
                in_specs=[pl.BlockSpec(block, lambda i, h: (i, 0, 0))] * 2
                + [pl.BlockSpec(memory_space=pl.ANY)] * len(before),
                out_specs=pl.BlockSpec(block, lambda i, h: (i, h[0], 0)),
            ),
            out_shape=jax.ShapeDtypeStruct((9, panel, outs), jnp.float32),
            input_output_aliases={3: 0} if before else {},
            compiler_params=params,
            name="join",
        )(which, *terms, *before)

    grad_back = lax.all_to_all(back, "row", split_axis=0, concat_axis=0, tiled=True)
    grad_back, grad_weight = lax.optimization_barrier((grad_back, grad_weight))
    grad_in = pl.pallas_call(
        merge_kernel,
        grid=(2,),
        out_shape=jax.ShapeDtypeStruct((positions, in_chans), jnp.bfloat16),
        in_specs=[pl.BlockSpec((tiles, positions // 2, panel), lambda i: (0, i, 0))],
        out_specs=pl.BlockSpec((positions // 2, in_chans), lambda i: (i, 0)),
        compiler_params=params,
        name="merge",
    )(grad_back)

    return grad_in.reshape(rows, width, in_chans), grad_weight.reshape(3, 3, panel, outs)


def extended(x, sides, width):
    for axis, dim in sides:
        peers, length = (lax.axis_size(axis), x.shape[dim])
        up = [(i, (i + 1) % peers) for i in range(peers - 1)]
        down = [(j, i) for i, j in up]
        last = lax.slice_in_dim(x, length - width, length, axis=dim)
        initial = lax.slice_in_dim(x, 0, width, axis=dim)
        before = lax.ppermute(last, axis, up)
        after = lax.ppermute(initial, axis, down)
        x = jnp.concatenate([before, x, after], axis=dim)
    return x


def general(inputs, output_gradient, weight):
    height, width, in_chans = inputs.shape
    out_chans = output_gradient.shape[2]
    step = DILATION_STEP
    in_strip = lax.all_to_all(inputs, "row", split_axis=2, concat_axis=0, tiled=True)
    strip_rows = in_strip.shape[0]
    panel = in_strip.shape[2]
    in_padded = jnp.pad(in_strip, ((step, step), (0, 0), (0, 0)))
    side_rimmed = extended(output_gradient, (("col", 1),), step)
    piece = lax.all_gather(side_rimmed, "row", axis=0, tiled=True)
    start = jnp.int32(0)
    grad_padded = jnp.zeros((strip_rows + 2 * step, width, panel), jnp.float32)
    count = piece.shape[0]
    new_terms = []
    for kernel_tap_row in range(3):
        in_rows = lax.dynamic_slice_in_dim(in_padded, step * kernel_tap_row, count, 0).reshape(
            count * width, panel
        )
        back = jnp.zeros((count * width, panel), jnp.float32)
        for kernel_tap_column in range(3):
            left_offset = step * (2 - kernel_tap_column)
            window = piece[:, left_offset : left_offset + width, :].reshape(
                count * width, out_chans
            )
            new_terms.append(
                lax.dot_general(
                    in_rows, window, (((0,), (0,)), ((), ())), preferred_element_type=jnp.float32
                )
            )
            back = back + lax.dot_general(
                window,
                weight[kernel_tap_row, kernel_tap_column],
                (((1,), (1,)), ((), ())),
                preferred_element_type=jnp.float32,
            )
        target = start + step * kernel_tap_row
        current = lax.dynamic_slice_in_dim(grad_padded, target, count, 0)
        grad_padded = lax.dynamic_update_slice_in_dim(
            grad_padded, current + back.reshape(count, width, panel), target, 0
        )
    terms = jnp.stack(new_terms).reshape(3, 3, panel, out_chans)
    terms, grad_padded = (terms, grad_padded)
    grad_strip = grad_padded[step : step + strip_rows].astype(jnp.bfloat16)
    grad_in = lax.all_to_all(grad_strip, "row", split_axis=0, concat_axis=2, tiled=True)
    scale = 1.0 / math.sqrt(height * width * lax.axis_size("row") * lax.axis_size("col"))
    terms = terms * scale
    grad_weight = lax.psum(terms, "col")
    return (grad_in, grad_weight)


def shards(inputs, output_gradient, weight):
    rows, width, in_chans = inputs.shape
    tiles, strips = lax.axis_size("row"), lax.axis_size("col")
    fits = (
        tiles == 8
        and strips == 4
        and DILATION_STEP % rows == 0
        and DILATION_STEP <= width
        and width % 16 == 0
        and in_chans % (tiles * 256) == 0
        and output_gradient.shape[2] % 128 == 0
    )
    return (quick if fits else general)(inputs, output_gradient, weight)


def solution(mesh):
    return jax.shard_map(
        shards,
        mesh=mesh,
        in_specs=(P("row", "col", None), P("row", "col", None), P(None, None, "row", None)),
        out_specs=(P("row", "col", None), P(None, None, "row", None)),
        check_vma=False,
    )
```

```python
import math

import jax
import jax.numpy as jnp
from jax import lax
from jax.experimental import pallas as pl
from jax.experimental.pallas import tpu as pltpu
from jax.sharding import PartitionSpec as P

DILATION_STEP = 12
VMEM_LIMIT = 32 * 1024 * 1024


def swap(x, axis, bit):
    return lax.ppermute(x, axis, [(i, i ^ bit) for i in range(lax.axis_size(axis))])


def rims(x, width, core):
    peers, length = lax.axis_size("col"), x.shape[-2]
    first, last = x[..., :width, :], x[..., length - width :, :]
    near = swap(jnp.where(core == 0, last, first), "col", 1)
    pairs = [(i, i + 1) for i in range(1, peers - 1, 2)]
    beside = lax.ppermute(
        jnp.where(core == 0, first, last), "col", pairs + [(j, i) for i, j in pairs]
    )
    return near, beside


def split_kernel(me_ref, in_ref, own_ref, stay_ref, go_ref, go_far_ref):
    zs, _, panel = stay_ref.shape

    def channels(owner):
        return in_ref[:, pl.ds(pl.multiple_of(owner * panel, 128), panel)]

    for k in range(zs):
        owner = me_ref[0] ^ (2 * k)
        stay_ref[k] = channels(owner)
        if k < zs // 2:
            go_ref[k] = channels(owner ^ 1)
        else:
            go_far_ref[k - zs // 2] = channels(owner ^ 1)
    go_ref[zs // 2] = own_ref[...]


def pack_kernel(first, stay_ref, got_ref, *out_refs):
    for k, out_ref in enumerate(out_refs):
        out_ref[0] = stay_ref[first + k]
        out_ref[1] = got_ref[k]


def merge_kernel(block_ref, out_ref):
    tiles, _, chans = block_ref.shape
    for t in range(tiles):
        out_ref[:, t * chans : (t + 1) * chans] = block_ref[t]


def start_all(copies):
    for copy in copies:
        copy.start()
    return copies


def wait_all(copies):
    for copy in copies:
        copy.wait()


def piece_copies(piece_refs, tile_ref, near_ref, beside_ref, sem):
    own_ref, got_ref, rest_ref, rest_y_ref, near_from, beside_from = piece_refs
    tiles = tile_ref.shape[0]
    copies = []
    for k in range(tiles):
        if k < 2:
            source = got_ref.at[got_ref.shape[0] - 1] if k else own_ref
        else:
            source = (rest_y_ref if k % 2 else rest_ref).at[k // 2 - 1]
        copies.append(pltpu.make_async_copy(source, tile_ref.at[k], sem.at[k]))
    copies.append(pltpu.make_async_copy(near_from, near_ref, sem.at[tiles]))
    copies.append(pltpu.make_async_copy(beside_from, beside_ref, sem.at[tiles + 1]))
    return copies


def windows_of(me, core, tile_ref, near_ref, beside_ref, windows_ref):
    tiles, positions, outs = tile_ref.shape
    rows, step = near_ref.shape[1:3]
    width = positions // rows
    pad = (windows_ref.shape[0] - tiles) // 2
    zeros = jnp.zeros(windows_ref.shape[1:], windows_ref.dtype)
    for k in range(pad):
        windows_ref[k] = zeros
        windows_ref[pad + tiles + k] = zeros
    for k in range(tiles):
        tile = tile_ref[k].reshape(rows, width, outs)
        at = k if k < 2 else k // 2 + 1 + k % 2 * (tiles // 2 - 1)
        tile, near, beside = (
            v.astype(jnp.float32) for v in (tile, near_ref[at], beside_ref[at])
        )
        left = jnp.where(core == 0, beside, near)
        right = jnp.where(core == 0, near, beside)
        shifted = (
            jnp.concatenate([tile[:, step:], right], axis=1),
            tile,
            jnp.concatenate([left, tile[:, : width - step]], axis=1),
        )
        for b in range(3):
            windows_ref[pad + (me ^ k), :, b * outs : (b + 1) * outs] = (
                shifted[b].reshape(positions, outs).astype(jnp.bfloat16)
            )


def windows_kernel(me_ref, core_ref, *refs):
    piece_refs, windows_ref = refs[:6], refs[6]
    tile_ref, near_ref, beside_ref, sem = refs[7:]
    wait_all(start_all(piece_copies(piece_refs, tile_ref, near_ref, beside_ref, sem)))
    windows_of(me_ref[0], core_ref[0], tile_ref, near_ref, beside_ref, windows_ref)


def back_kernel(shift, windows_ref, weight_ref, back_ref, flat_ref):
    tiles, depth = back_ref.shape[0], windows_ref.shape[2]
    outs = weight_ref.shape[2]
    for t in range(weight_ref.shape[0]):
        flat_ref[:, t * outs : (t + 1) * outs] = weight_ref[t]
    for j in range(tiles):
        taps = [a for a in range(3) if 0 <= j - shift * (a - 1) < tiles]
        lhs = jnp.concatenate([windows_ref[j - shift * (a - 2)] for a in taps], axis=1)
        rhs = flat_ref[:, taps[0] * depth : (taps[-1] + 1) * depth]
        back_ref[j] = lax.dot_general(
            lhs, rhs, (((1,), (1,)), ((), ())), preferred_element_type=jnp.float32
        ).astype(back_ref.dtype)


def terms_of(pad, scale, flipped, windows_ref, out_ref):
    positions, outs = windows_ref.shape[1], out_ref.shape[2]
    tiles = flipped.shape[1] // positions
    for a in range(3):
        move = pad * (a - 1)
        first, last = max(0, move), min(tiles, tiles + move)
        lhs = flipped[:, first * positions : last * positions]
        rhs = windows_ref[pad + first - move : pad + last - move].reshape(
            (last - first) * positions, 3 * outs
        )
        terms = jnp.dot(lhs, rhs, preferred_element_type=jnp.float32) * scale
        for b in range(3):
            out_ref[3 * a + b] = terms[:, b * outs : (b + 1) * outs]


def other_kernel(pad, scale, me_ref, core_ref, *refs):
    *strip_from, windows_ref, other_ref, mine_ref, strip_ref, flipped_ref, sem = refs
    tiles, positions, chans = strip_ref.shape
    half = chans // 2
    core, me = core_ref[0], me_ref[0]
    wait_all(
        start_all(
            [
                pltpu.make_async_copy(ref, strip_ref.at[pl.ds(2 * k, 2)], sem.at[k])
                for k, ref in enumerate(strip_from)
            ]
        )
    )
    for j in range(tiles):
        x = strip_ref[me ^ j]
        low, high = x[:, :half], x[:, half:]
        columns = slice(j * positions, (j + 1) * positions)
        mine_ref[:, columns] = jnp.where(core == 0, low, high).T
        flipped_ref[:, columns] = jnp.where(core == 0, high, low).T
    terms_of(pad, scale, flipped_ref, windows_ref, other_ref)


def mine_kernel(pad, scale, flipped_ref, windows_ref, mine_ref):
    terms_of(pad, scale, flipped_ref, windows_ref, mine_ref)


def join_kernel(half_ref, part_ref, part_x_ref, *refs):
    refs[-1][...] = part_ref[...] + part_x_ref[...]


def vmem(n):
    return [pl.BlockSpec(memory_space=pltpu.VMEM)] * n


def whole(*arrays):
    return [pl.BlockSpec(a.shape, lambda i, n=a.ndim: (0,) * n) for a in arrays]


def quick(inputs, output_gradient, weight):
    rows, width, in_chans = inputs.shape
    outs = output_gradient.shape[2]
    tiles = lax.axis_size("row")
    panel = in_chans // tiles
    positions = rows * width
    shift = DILATION_STEP // rows
    me = lax.axis_index("row").astype(jnp.int32).reshape(1)
    core = (lax.axis_index("col") % 2).astype(jnp.int32).reshape(1)
    params = pltpu.CompilerParams(vmem_limit_bytes=VMEM_LIMIT)
    smem = pl.BlockSpec(memory_space=pltpu.SMEM)

    zs = tiles // 2
    flat = inputs.reshape(positions, in_chans)
    sizes = (zs, zs // 2 + 1, zs // 2)
    stay, go, go_far = pl.pallas_call(
        split_kernel,
        grid=(2,),
        out_shape=[jax.ShapeDtypeStruct((n, positions, panel), jnp.bfloat16) for n in sizes],
        in_specs=[
            smem,
            pl.BlockSpec((positions // 2, in_chans), lambda i: (i, 0)),
            pl.BlockSpec((positions // 2, outs), lambda i: (i, 0)),
        ],
        out_specs=[pl.BlockSpec((n, positions // 2, panel), lambda i: (0, i, 0)) for n in sizes],
        compiler_params=params,
        name="split",
    )(me, flat, output_gradient.reshape(positions, outs))
    own = output_gradient.reshape(positions, outs)
    got_far = swap(go_far, "row", 1)
    got = swap(go, "row", 1)

    def pack(first, arrived):
        count = zs // 2
        return pl.pallas_call(
            lambda *refs: pack_kernel(first, *refs),
            grid=(1,),
            out_shape=[jax.ShapeDtypeStruct((2, positions, panel), jnp.bfloat16)] * count,
            in_specs=whole(stay, arrived),
            out_specs=[pl.BlockSpec((2, positions, panel), lambda i: (0, 0, 0))] * count,
            compiler_params=params,
            name="pack",
        )(stay, arrived)

    far_pairs = pack(zs // 2, got_far)
    far = swap(own, "row", 4)
    far, *far_pairs = lax.optimization_barrier((far, *far_pairs))
    rest = jnp.stack([swap(own, "row", 2), far, swap(far, "row", 2)])
    pairs = [*pack(0, got), *far_pairs]
    strip = [p if k == 0 else swap(p, "row", 2 * k) for k, p in enumerate(pairs)]

    rest_y = swap(rest, "row", 1)
    stacked = jnp.concatenate([own[None], got[zs // 2 :], rest, rest_y])
    near, beside = rims(stacked.reshape(tiles, rows, width, outs), DILATION_STEP, core)

    pieces = (own, got, rest, rest_y, near, beside)
    hbm = pl.BlockSpec(memory_space=pltpu.HBM)
    windows = pl.pallas_call(
        windows_kernel,
        out_shape=jax.ShapeDtypeStruct((tiles + 2 * shift, positions, 3 * outs), jnp.bfloat16),
        in_specs=[smem, smem] + [hbm] * 6,
        out_specs=vmem(1)[0],
        scratch_shapes=[
            pltpu.VMEM((tiles, positions, outs), jnp.bfloat16),
            pltpu.VMEM(near.shape, jnp.bfloat16),
            pltpu.VMEM(beside.shape, jnp.bfloat16),
            pltpu.SemaphoreType.DMA((tiles + 2,)),
        ],
        compiler_params=params,
        name="windows",
    )(me, core, *pieces)
    scale = 1.0 / math.sqrt(rows * tiles * width * lax.axis_size("col"))
    half = jax.ShapeDtypeStruct((9, panel // 2, outs), jnp.float32)
    theirs, flipped = pl.pallas_call(
        lambda *refs: other_kernel(shift, scale, *refs),
        out_shape=(half, jax.ShapeDtypeStruct((panel // 2, tiles * positions), jnp.bfloat16)),
        in_specs=[smem, smem] + [hbm] * zs + vmem(1),
        out_specs=tuple(vmem(2)),
        scratch_shapes=[
            pltpu.VMEM((tiles, positions, panel), jnp.bfloat16),
            pltpu.VMEM((panel // 2, tiles * positions), jnp.bfloat16),
            pltpu.SemaphoreType.DMA((zs,)),
        ],
        compiler_params=params,
        name="other_terms",
    )(me, core, *strip, windows)
    weight, theirs = lax.optimization_barrier((weight, theirs))
    back = pl.pallas_call(
        lambda *refs: back_kernel(shift, *refs),
        out_shape=jax.ShapeDtypeStruct((tiles, positions, panel), jnp.bfloat16),
        in_specs=vmem(2),
        out_specs=vmem(1)[0],
        scratch_shapes=[pltpu.VMEM((panel, 9 * outs), jnp.bfloat16)],
        compiler_params=params,
        name="back",
    )(windows, weight.reshape(9, panel, outs))
    mine = pl.pallas_call(
        lambda *refs: mine_kernel(shift, scale, *refs),
        out_shape=half,
        in_specs=vmem(2),
        out_specs=vmem(1)[0],
        compiler_params=params,
        name="mine_terms",
    )(flipped, windows)
    chip = mine + swap(theirs, "col", 1)
    chip, back = lax.optimization_barrier((chip, back))
    across = swap(chip, "col", 2)
    other = (swap(chip, "col", 1), swap(across, "col", 1))
    grad_weight = None
    for which, terms in ((core, (chip, across)), (1 - core, other)):
        before = [] if grad_weight is None else [grad_weight]
        block = (3, panel // 2, outs)
        grad_weight = pl.pallas_call(
            join_kernel,
            grid_spec=pltpu.PrefetchScalarGridSpec(
                num_scalar_prefetch=1,
                grid=(3,),
                in_specs=[pl.BlockSpec(block, lambda i, h: (i, 0, 0))] * 2
                + [pl.BlockSpec(memory_space=pl.ANY)] * len(before),
                out_specs=pl.BlockSpec(block, lambda i, h: (i, h[0], 0)),
            ),
            out_shape=jax.ShapeDtypeStruct((9, panel, outs), jnp.float32),
            input_output_aliases={3: 0} if before else {},
            compiler_params=params,
            name="join",
        )(which, *terms, *before)

    grad_back = lax.all_to_all(back, "row", split_axis=0, concat_axis=0, tiled=True)
    grad_back, grad_weight = lax.optimization_barrier((grad_back, grad_weight))
    grad_in = pl.pallas_call(
        merge_kernel,
        grid=(2,),
        out_shape=jax.ShapeDtypeStruct((positions, in_chans), jnp.bfloat16),
        in_specs=[pl.BlockSpec((tiles, positions // 2, panel), lambda i: (0, i, 0))],
        out_specs=pl.BlockSpec((positions // 2, in_chans), lambda i: (i, 0)),
        compiler_params=params,
        name="merge",
    )(grad_back)

    return grad_in.reshape(rows, width, in_chans), grad_weight.reshape(3, 3, panel, outs)


def extended(x, sides, width):
    for axis, dim in sides:
        peers, length = (lax.axis_size(axis), x.shape[dim])
        up = [(i, (i + 1) % peers) for i in range(peers - 1)]
        down = [(j, i) for i, j in up]
        last = lax.slice_in_dim(x, length - width, length, axis=dim)
        initial = lax.slice_in_dim(x, 0, width, axis=dim)
        before = lax.ppermute(last, axis, up)
        after = lax.ppermute(initial, axis, down)
        x = jnp.concatenate([before, x, after], axis=dim)
    return x


def general(inputs, output_gradient, weight):
    height, width, in_chans = inputs.shape
    out_chans = output_gradient.shape[2]
    step = DILATION_STEP
    in_strip = lax.all_to_all(inputs, "row", split_axis=2, concat_axis=0, tiled=True)
    strip_rows = in_strip.shape[0]
    panel = in_strip.shape[2]
    in_padded = jnp.pad(in_strip, ((step, step), (0, 0), (0, 0)))
    side_rimmed = extended(output_gradient, (("col", 1),), step)
    piece = lax.all_gather(side_rimmed, "row", axis=0, tiled=True)
    start = jnp.int32(0)
    grad_padded = jnp.zeros((strip_rows + 2 * step, width, panel), jnp.float32)
    count = piece.shape[0]
    new_terms = []
    for kernel_tap_row in range(3):
        in_rows = lax.dynamic_slice_in_dim(in_padded, step * kernel_tap_row, count, 0).reshape(
            count * width, panel
        )
        back = jnp.zeros((count * width, panel), jnp.float32)
        for kernel_tap_column in range(3):
            left_offset = step * (2 - kernel_tap_column)
            window = piece[:, left_offset : left_offset + width, :].reshape(
                count * width, out_chans
            )
            new_terms.append(
                lax.dot_general(
                    in_rows, window, (((0,), (0,)), ((), ())), preferred_element_type=jnp.float32
                )
            )
            back = back + lax.dot_general(
                window,
                weight[kernel_tap_row, kernel_tap_column],
                (((1,), (1,)), ((), ())),
                preferred_element_type=jnp.float32,
            )
        target = start + step * kernel_tap_row
        current = lax.dynamic_slice_in_dim(grad_padded, target, count, 0)
        grad_padded = lax.dynamic_update_slice_in_dim(
            grad_padded, current + back.reshape(count, width, panel), target, 0
        )
    terms = jnp.stack(new_terms).reshape(3, 3, panel, out_chans)
    terms, grad_padded = (terms, grad_padded)
    grad_strip = grad_padded[step : step + strip_rows].astype(jnp.bfloat16)
    grad_in = lax.all_to_all(grad_strip, "row", split_axis=0, concat_axis=2, tiled=True)
    scale = 1.0 / math.sqrt(height * width * lax.axis_size("row") * lax.axis_size("col"))
    terms = terms * scale
    grad_weight = lax.psum(terms, "col")
    return (grad_in, grad_weight)


def shards(inputs, output_gradient, weight):
    rows, width, in_chans = inputs.shape
    tiles, strips = lax.axis_size("row"), lax.axis_size("col")
    fits = (
        tiles == 8
        and strips == 4
        and DILATION_STEP % rows == 0
        and DILATION_STEP <= width
        and width % 16 == 0
        and in_chans % (tiles * 256) == 0
        and output_gradient.shape[2] % 128 == 0
    )
    return (quick if fits else general)(inputs, output_gradient, weight)


def solution(mesh):
    return jax.shard_map(
        shards,
        mesh=mesh,
        in_specs=(P("row", "col", None), P("row", "col", None), P(None, None, "row", None)),
        out_specs=(P("row", "col", None), P(None, None, "row", None)),
        check_vma=False,
    )
```

```python
import math

import jax
import jax.numpy as jnp
from jax import lax
from jax.experimental import pallas as pl
from jax.experimental.pallas import tpu as pltpu
from jax.sharding import PartitionSpec as P

DILATION_STEP = 12
VMEM_LIMIT = 32 * 1024 * 1024


def swap(x, axis, bit):
    return lax.ppermute(x, axis, [(i, i ^ bit) for i in range(lax.axis_size(axis))])


def rims(x, width, core):
    peers, length = lax.axis_size("col"), x.shape[-2]
    first, last = x[..., :width, :], x[..., length - width :, :]
    near = swap(jnp.where(core == 0, last, first), "col", 1)
    pairs = [(i, i + 1) for i in range(1, peers - 1, 2)]
    beside = lax.ppermute(
        jnp.where(core == 0, first, last), "col", pairs + [(j, i) for i, j in pairs]
    )
    return near, beside


def split_kernel(me_ref, in_ref, own_ref, stay_ref, go_own_ref, go_near_ref, go_far_ref):
    zs, _, panel = stay_ref.shape

    def channels(owner):
        return in_ref[:, pl.ds(pl.multiple_of(owner * panel, 128), panel)]

    targets = [go_own_ref.at[0], go_near_ref.at[0], go_far_ref.at[0], go_far_ref.at[1]]
    for k in range(zs):
        owner = me_ref[0] ^ (2 * k)
        stay_ref[k] = channels(owner)
        targets[k][...] = channels(owner ^ 1)
    go_near_ref[1] = own_ref[...]


def pack_kernel(first, stay_ref, got_ref, *out_refs):
    for k, out_ref in enumerate(out_refs):
        out_ref[0] = stay_ref[first + k]
        out_ref[1] = got_ref[k]


def merge_kernel(block_ref, out_ref):
    tiles, _, chans = block_ref.shape
    for t in range(tiles):
        out_ref[:, t * chans : (t + 1) * chans] = block_ref[t]


def start_all(copies):
    for copy in copies:
        copy.start()
    return copies


def wait_all(copies):
    for copy in copies:
        copy.wait()


def piece_copies(piece_refs, tile_ref, near_ref, beside_ref, sem):
    own_ref, got_ref, rest_ref, rest_y_ref, *relayed_refs, near_from, beside_from = piece_refs
    tiles = tile_ref.shape[0]
    copies = []
    for k in range(tiles):
        if k < 2:
            source = got_ref.at[got_ref.shape[0] - 1] if k else own_ref
        elif k < tiles - 2:
            source = (rest_y_ref if k % 2 else rest_ref).at[k // 2 - 1]
        else:
            source = relayed_refs[k % 2]
        copies.append(pltpu.make_async_copy(source, tile_ref.at[k], sem.at[k]))
    copies.append(pltpu.make_async_copy(near_from, near_ref, sem.at[tiles]))
    copies.append(pltpu.make_async_copy(beside_from, beside_ref, sem.at[tiles + 1]))
    return copies


def windows_of(me, core, tile_ref, near_ref, beside_ref, windows_ref):
    tiles, positions, outs = tile_ref.shape
    rows, step = near_ref.shape[1:3]
    width = positions // rows
    pad = (windows_ref.shape[0] - tiles) // 2
    for k in range(tiles):
        tile = tile_ref[k].reshape(rows, width, outs)
        at = k if k < 2 else k // 2 + 1 + k % 2 * (tiles // 2 - 1)
        tile, near, beside = (
            v.astype(jnp.float32) for v in (tile, near_ref[at], beside_ref[at])
        )
        left = jnp.where(core == 0, beside, near)
        right = jnp.where(core == 0, near, beside)
        shifted = (
            jnp.concatenate([tile[:, step:], right], axis=1),
            tile,
            jnp.concatenate([left, tile[:, : width - step]], axis=1),
        )
        for b in range(3):
            windows_ref[pad + (me ^ k), :, b * outs : (b + 1) * outs] = (
                shifted[b].reshape(positions, outs).astype(jnp.bfloat16)
            )


def windows_kernel(me_ref, core_ref, *refs):
    piece_refs, windows_ref = refs[:8], refs[8]
    tile_ref, near_ref, beside_ref, sem = refs[9:]
    wait_all(start_all(piece_copies(piece_refs, tile_ref, near_ref, beside_ref, sem)))
    windows_of(me_ref[0], core_ref[0], tile_ref, near_ref, beside_ref, windows_ref)


def back_kernel(shift, windows_ref, weight_ref, back_ref, flat_ref):
    tiles, positions, chans = back_ref.shape
    depth, outs = windows_ref.shape[2], weight_ref.shape[2]
    for t in range(weight_ref.shape[0]):
        flat_ref[:, t * outs : (t + 1) * outs] = weight_ref[t]
    reach = [[a for a in range(3) if 0 <= j - shift * (a - 1) < tiles] for j in range(tiles)]
    first = 0
    while first < tiles:
        taps, last = reach[first], first + 1
        while last < tiles and reach[last] == taps:
            last += 1
        lhs = jnp.concatenate(
            [
                windows_ref[pl.ds(shift + first - shift * (a - 1), last - first)].reshape(
                    (last - first) * positions, depth
                )
                for a in taps
            ],
            axis=1,
        )
        rhs = flat_ref[:, taps[0] * depth : (taps[-1] + 1) * depth]
        product = lax.dot_general(
            lhs, rhs, (((1,), (1,)), ((), ())), preferred_element_type=jnp.float32
        )
        back_ref[pl.ds(first, last - first)] = product.astype(back_ref.dtype).reshape(
            last - first, positions, chans
        )
        first = last


def terms_of(pad, scale, flipped, windows_ref, out_ref):
    positions, outs = windows_ref.shape[1], out_ref.shape[2]
    tiles = flipped.shape[1] // positions
    for a in range(3):
        move = pad * (a - 1)
        first, last = max(0, move), min(tiles, tiles + move)
        lhs = flipped[:, first * positions : last * positions]
        rhs = windows_ref[pad + first - move : pad + last - move].reshape(
            (last - first) * positions, 3 * outs
        )
        terms = jnp.dot(lhs, rhs, preferred_element_type=jnp.float32) * scale
        for b in range(3):
            out_ref[3 * a + b] = terms[:, b * outs : (b + 1) * outs]


def other_kernel(pad, scale, me_ref, core_ref, *refs):
    *strip_from, windows_ref, other_ref, mine_ref, strip_ref, flipped_ref, sem = refs
    tiles, positions, chans = strip_ref.shape
    half = chans // 2
    core, me = core_ref[0], me_ref[0]
    stay_ref, got_ref, *pair_refs = strip_from
    places = [(stay_ref.at[pl.ds(0, 1)], 0, 1), (got_ref, 1, 1)]
    places += [(ref, 2 * k, 2) for k, ref in enumerate(pair_refs, 1)]
    wait_all(
        start_all(
            [
                pltpu.make_async_copy(ref, strip_ref.at[pl.ds(first, count)], sem.at[n])
                for n, (ref, first, count) in enumerate(places)
            ]
        )
    )
    for j in range(tiles):
        x = strip_ref[me ^ j]
        low, high = x[:, :half], x[:, half:]
        columns = slice(j * positions, (j + 1) * positions)
        mine_ref[:, columns] = jnp.where(core == 0, low, high).T
        flipped_ref[:, columns] = jnp.where(core == 0, high, low).T
    terms_of(pad, scale, flipped_ref, windows_ref, other_ref)


def mine_kernel(pad, scale, flipped_ref, windows_ref, mine_ref):
    terms_of(pad, scale, flipped_ref, windows_ref, mine_ref)


def join_kernel(half_ref, part_ref, part_x_ref, *refs):
    refs[-1][...] = part_ref[...] + part_x_ref[...]


def vmem(n):
    return [pl.BlockSpec(memory_space=pltpu.VMEM)] * n


def whole(*arrays):
    return [pl.BlockSpec(a.shape, lambda i, n=a.ndim: (0,) * n) for a in arrays]


def quick(inputs, output_gradient, weight):
    rows, width, in_chans = inputs.shape
    outs = output_gradient.shape[2]
    tiles = lax.axis_size("row")
    panel = in_chans // tiles
    positions = rows * width
    shift = DILATION_STEP // rows
    me = lax.axis_index("row").astype(jnp.int32).reshape(1)
    core = (lax.axis_index("col") % 2).astype(jnp.int32).reshape(1)
    params = pltpu.CompilerParams(vmem_limit_bytes=VMEM_LIMIT)
    smem = pl.BlockSpec(memory_space=pltpu.SMEM)

    zs = tiles // 2
    flat = inputs.reshape(positions, in_chans)
    sizes = (zs, 1, 2, 2)
    stay, go_own, go_near, go_far = pl.pallas_call(
        split_kernel,
        grid=(2,),
        out_shape=[jax.ShapeDtypeStruct((n, positions, panel), jnp.bfloat16) for n in sizes],
        in_specs=[
            smem,
            pl.BlockSpec((positions // 2, in_chans), lambda i: (i, 0)),
            pl.BlockSpec((positions // 2, outs), lambda i: (i, 0)),
        ],
        out_specs=[pl.BlockSpec((n, positions // 2, panel), lambda i: (0, i, 0)) for n in sizes],
        compiler_params=params,
        name="split",
    )(me, flat, output_gradient.reshape(positions, outs))
    own = output_gradient.reshape(positions, outs)
    got_far = swap(go_far, "row", 1)
    got = swap(go_near, "row", 1)

    def pack(first, count, arrived):
        return pl.pallas_call(
            lambda *refs: pack_kernel(first, *refs),
            grid=(1,),
            out_shape=[jax.ShapeDtypeStruct((2, positions, panel), jnp.bfloat16)] * count,
            in_specs=whole(stay, arrived),
            out_specs=[pl.BlockSpec((2, positions, panel), lambda i: (0, 0, 0))] * count,
            compiler_params=params,
            name="pack",
        )(stay, arrived)

    far_pairs = pack(2, 2, got_far)
    far = swap(own, "row", 4)
    far, *far_pairs = lax.optimization_barrier((far, *far_pairs))
    rest = jnp.stack([swap(own, "row", 2), far])
    relayed = swap(far, "row", 2)
    pairs = [*pack(1, 1, got), *far_pairs]
    got_own = swap(go_own, "row", 1)
    strip = [stay, got_own] + [swap(p, "row", 2 * k) for k, p in enumerate(pairs, 1)]

    relayed, strip[1] = lax.optimization_barrier((relayed, strip[1]))
    rest_y = swap(rest, "row", 1)
    relayed_y = swap(relayed, "row", 1)
    stacked = jnp.concatenate([own[None], got[1:], rest, relayed[None], rest_y, relayed_y[None]])
    near, beside = rims(stacked.reshape(tiles, rows, width, outs), DILATION_STEP, core)

    pieces = (own, got, rest, rest_y, relayed, relayed_y, near, beside)
    hbm = pl.BlockSpec(memory_space=pltpu.HBM)
    windows = pl.pallas_call(
        windows_kernel,
        out_shape=jax.ShapeDtypeStruct((tiles + 2 * shift, positions, 3 * outs), jnp.bfloat16),
        in_specs=[smem, smem] + [hbm] * 8,
        out_specs=vmem(1)[0],
        scratch_shapes=[
            pltpu.VMEM((tiles, positions, outs), jnp.bfloat16),
            pltpu.VMEM(near.shape, jnp.bfloat16),
            pltpu.VMEM(beside.shape, jnp.bfloat16),
            pltpu.SemaphoreType.DMA((tiles + 2,)),
        ],
        compiler_params=params,
        name="windows",
    )(me, core, *pieces)
    scale = 1.0 / math.sqrt(rows * tiles * width * lax.axis_size("col"))
    half = jax.ShapeDtypeStruct((9, panel // 2, outs), jnp.float32)
    theirs, flipped = pl.pallas_call(
        lambda *refs: other_kernel(shift, scale, *refs),
        out_shape=(half, jax.ShapeDtypeStruct((panel // 2, tiles * positions), jnp.bfloat16)),
        in_specs=[smem, smem] + [hbm] * (zs + 1) + vmem(1),
        out_specs=tuple(vmem(2)),
        scratch_shapes=[
            pltpu.VMEM((tiles, positions, panel), jnp.bfloat16),
            pltpu.VMEM((panel // 2, tiles * positions), jnp.bfloat16),
            pltpu.SemaphoreType.DMA((zs + 1,)),
        ],
        compiler_params=params,
        name="other_terms",
    )(me, core, *strip, windows)
    weight, theirs = lax.optimization_barrier((weight, theirs))
    back = pl.pallas_call(
        lambda *refs: back_kernel(shift, *refs),
        out_shape=jax.ShapeDtypeStruct((tiles, positions, panel), jnp.bfloat16),
        in_specs=vmem(2),
        out_specs=vmem(1)[0],
        scratch_shapes=[pltpu.VMEM((panel, 9 * outs), jnp.bfloat16)],
        compiler_params=params,
        name="back",
    )(windows, weight.reshape(9, panel, outs))
    mine = pl.pallas_call(
        lambda *refs: mine_kernel(shift, scale, *refs),
        out_shape=half,
        in_specs=vmem(2),
        out_specs=vmem(1)[0],
        compiler_params=params,
        name="mine_terms",
    )(flipped, windows)
    chip = mine + swap(theirs, "col", 1)
    chip, back = lax.optimization_barrier((chip, back))
    across = swap(chip, "col", 2)
    other = (swap(chip, "col", 1), swap(across, "col", 1))
    grad_weight = None
    for which, terms in ((core, (chip, across)), (1 - core, other)):
        before = [] if grad_weight is None else [grad_weight]
        block = (3, panel // 2, outs)
        grad_weight = pl.pallas_call(
            join_kernel,
            grid_spec=pltpu.PrefetchScalarGridSpec(
                num_scalar_prefetch=1,
                grid=(3,),
                in_specs=[pl.BlockSpec(block, lambda i, h: (i, 0, 0))] * 2
                + [pl.BlockSpec(memory_space=pl.ANY)] * len(before),
                out_specs=pl.BlockSpec(block, lambda i, h: (i, h[0], 0)),
            ),
            out_shape=jax.ShapeDtypeStruct((9, panel, outs), jnp.float32),
            input_output_aliases={3: 0} if before else {},
            compiler_params=params,
            name="join",
        )(which, *terms, *before)

    grad_back = lax.all_to_all(back, "row", split_axis=0, concat_axis=0, tiled=True)
    grad_back, grad_weight = lax.optimization_barrier((grad_back, grad_weight))
    grad_in = pl.pallas_call(
        merge_kernel,
        grid=(2,),
        out_shape=jax.ShapeDtypeStruct((positions, in_chans), jnp.bfloat16),
        in_specs=[pl.BlockSpec((tiles, positions // 2, panel), lambda i: (0, i, 0))],
        out_specs=pl.BlockSpec((positions // 2, in_chans), lambda i: (i, 0)),
        compiler_params=params,
        name="merge",
    )(grad_back)

    return grad_in.reshape(rows, width, in_chans), grad_weight.reshape(3, 3, panel, outs)


def extended(x, sides, width):
    for axis, dim in sides:
        peers, length = (lax.axis_size(axis), x.shape[dim])
        up = [(i, (i + 1) % peers) for i in range(peers - 1)]
        down = [(j, i) for i, j in up]
        last = lax.slice_in_dim(x, length - width, length, axis=dim)
        initial = lax.slice_in_dim(x, 0, width, axis=dim)
        before = lax.ppermute(last, axis, up)
        after = lax.ppermute(initial, axis, down)
        x = jnp.concatenate([before, x, after], axis=dim)
    return x


def general(inputs, output_gradient, weight):
    height, width, in_chans = inputs.shape
    out_chans = output_gradient.shape[2]
    step = DILATION_STEP
    in_strip = lax.all_to_all(inputs, "row", split_axis=2, concat_axis=0, tiled=True)
    strip_rows = in_strip.shape[0]
    panel = in_strip.shape[2]
    in_padded = jnp.pad(in_strip, ((step, step), (0, 0), (0, 0)))
    side_rimmed = extended(output_gradient, (("col", 1),), step)
    piece = lax.all_gather(side_rimmed, "row", axis=0, tiled=True)
    start = jnp.int32(0)
    grad_padded = jnp.zeros((strip_rows + 2 * step, width, panel), jnp.float32)
    count = piece.shape[0]
    new_terms = []
    for kernel_tap_row in range(3):
        in_rows = lax.dynamic_slice_in_dim(in_padded, step * kernel_tap_row, count, 0).reshape(
            count * width, panel
        )
        back = jnp.zeros((count * width, panel), jnp.float32)
        for kernel_tap_column in range(3):
            left_offset = step * (2 - kernel_tap_column)
            window = piece[:, left_offset : left_offset + width, :].reshape(
                count * width, out_chans
            )
            new_terms.append(
                lax.dot_general(
                    in_rows, window, (((0,), (0,)), ((), ())), preferred_element_type=jnp.float32
                )
            )
            back = back + lax.dot_general(
                window,
                weight[kernel_tap_row, kernel_tap_column],
                (((1,), (1,)), ((), ())),
                preferred_element_type=jnp.float32,
            )
        target = start + step * kernel_tap_row
        current = lax.dynamic_slice_in_dim(grad_padded, target, count, 0)
        grad_padded = lax.dynamic_update_slice_in_dim(
            grad_padded, current + back.reshape(count, width, panel), target, 0
        )
    terms = jnp.stack(new_terms).reshape(3, 3, panel, out_chans)
    terms, grad_padded = (terms, grad_padded)
    grad_strip = grad_padded[step : step + strip_rows].astype(jnp.bfloat16)
    grad_in = lax.all_to_all(grad_strip, "row", split_axis=0, concat_axis=2, tiled=True)
    scale = 1.0 / math.sqrt(height * width * lax.axis_size("row") * lax.axis_size("col"))
    terms = terms * scale
    grad_weight = lax.psum(terms, "col")
    return (grad_in, grad_weight)


def shards(inputs, output_gradient, weight):
    rows, width, in_chans = inputs.shape
    tiles, strips = lax.axis_size("row"), lax.axis_size("col")
    fits = (
        tiles == 8
        and strips == 4
        and DILATION_STEP % rows == 0
        and DILATION_STEP <= width
        and width % 16 == 0
        and in_chans % (tiles * 256) == 0
        and output_gradient.shape[2] % 128 == 0
    )
    return (quick if fits else general)(inputs, output_gradient, weight)


def solution(mesh):
    return jax.shard_map(
        shards,
        mesh=mesh,
        in_specs=(P("row", "col", None), P("row", "col", None), P(None, None, "row", None)),
        out_specs=(P("row", "col", None), P(None, None, "row", None)),
        check_vma=False,
    )
```

```python
import math

import jax
import jax.numpy as jnp
from jax import lax
from jax.experimental import pallas as pl
from jax.experimental.pallas import tpu as pltpu
from jax.sharding import PartitionSpec as P

DILATION_STEP = 12
VMEM_LIMIT = 32 * 1024 * 1024


def swap(x, axis, bit):
    return lax.ppermute(x, axis, [(i, i ^ bit) for i in range(lax.axis_size(axis))])


def rims(x, width, core):
    peers, length = lax.axis_size("col"), x.shape[-2]
    first, last = x[..., :width, :], x[..., length - width :, :]
    near = swap(jnp.where(core == 0, last, first), "col", 1)
    pairs = [(i, i + 1) for i in range(1, peers - 1, 2)]
    beside = lax.ppermute(
        jnp.where(core == 0, first, last), "col", pairs + [(j, i) for i, j in pairs]
    )
    return near, beside


def split_kernel(me_ref, in_ref, own_ref, stay_ref, go_own_ref, go_near_ref, go_far_ref):
    zs, _, panel = stay_ref.shape

    def channels(owner):
        return in_ref[:, pl.ds(pl.multiple_of(owner * panel, 128), panel)]

    targets = [go_own_ref.at[0], go_near_ref.at[0], go_far_ref.at[0], go_far_ref.at[1]]
    for k in range(zs):
        owner = me_ref[0] ^ (2 * k)
        stay_ref[k] = channels(owner)
        targets[k][...] = channels(owner ^ 1)
    go_near_ref[1] = own_ref[...]


def pack_kernel(first, stay_ref, got_ref, *out_refs):
    for k, out_ref in enumerate(out_refs):
        out_ref[0] = stay_ref[first + k]
        out_ref[1] = got_ref[k]


def merge_kernel(block_ref, out_ref):
    tiles, _, chans = block_ref.shape
    for t in range(tiles):
        out_ref[:, t * chans : (t + 1) * chans] = block_ref[t]


def start_all(copies):
    for copy in copies:
        copy.start()
    return copies


def wait_all(copies):
    for copy in copies:
        copy.wait()


def piece_copies(piece_refs, tile_ref, near_ref, beside_ref, sem):
    own_ref, got_ref, rest_ref, rest_y_ref, *relayed_refs, near_from, beside_from = piece_refs
    tiles = tile_ref.shape[0]
    copies = []
    for k in range(tiles):
        if k < 2:
            source = got_ref.at[got_ref.shape[0] - 1] if k else own_ref
        elif k < tiles - 2:
            source = (rest_y_ref if k % 2 else rest_ref).at[k // 2 - 1]
        else:
            source = relayed_refs[k % 2]
        copies.append(pltpu.make_async_copy(source, tile_ref.at[k], sem.at[k]))
    copies.append(pltpu.make_async_copy(near_from, near_ref, sem.at[tiles]))
    copies.append(pltpu.make_async_copy(beside_from, beside_ref, sem.at[tiles + 1]))
    return copies


def windows_of(me, core, tile_ref, near_ref, beside_ref, windows_ref):
    tiles, positions, outs = tile_ref.shape
    rows, step = near_ref.shape[1:3]
    width = positions // rows
    pad = (windows_ref.shape[0] - tiles) // 2
    for k in range(tiles):
        tile = tile_ref[k].reshape(rows, width, outs)
        at = k if k < 2 else k // 2 + 1 + k % 2 * (tiles // 2 - 1)
        tile, near, beside = (
            v.astype(jnp.float32) for v in (tile, near_ref[at], beside_ref[at])
        )
        left = jnp.where(core == 0, beside, near)
        right = jnp.where(core == 0, near, beside)
        shifted = (
            jnp.concatenate([tile[:, step:], right], axis=1),
            tile,
            jnp.concatenate([left, tile[:, : width - step]], axis=1),
        )
        for b in range(3):
            windows_ref[pad + (me ^ k), :, b * outs : (b + 1) * outs] = (
                shifted[b].reshape(positions, outs).astype(jnp.bfloat16)
            )


def windows_kernel(me_ref, core_ref, *refs):
    piece_refs, windows_ref = refs[:8], refs[8]
    tile_ref, near_ref, beside_ref, sem = refs[9:]
    wait_all(start_all(piece_copies(piece_refs, tile_ref, near_ref, beside_ref, sem)))
    windows_of(me_ref[0], core_ref[0], tile_ref, near_ref, beside_ref, windows_ref)


def back_kernel(shift, windows_ref, weight_ref, back_ref, flat_ref):
    tiles, positions, chans = back_ref.shape
    depth, outs = windows_ref.shape[2], weight_ref.shape[2]
    for t in range(weight_ref.shape[0]):
        flat_ref[:, t * outs : (t + 1) * outs] = weight_ref[t]
    reach = [[a for a in range(3) if 0 <= j - shift * (a - 1) < tiles] for j in range(tiles)]
    first = 0
    while first < tiles:
        taps, last = reach[first], first + 1
        while last < tiles and reach[last] == taps:
            last += 1
        lhs = jnp.concatenate(
            [
                windows_ref[pl.ds(shift + first - shift * (a - 1), last - first)].reshape(
                    (last - first) * positions, depth
                )
                for a in taps
            ],
            axis=1,
        )
        rhs = flat_ref[:, taps[0] * depth : (taps[-1] + 1) * depth]
        product = lax.dot_general(
            lhs, rhs, (((1,), (1,)), ((), ())), preferred_element_type=jnp.float32
        )
        back_ref[pl.ds(first, last - first)] = product.astype(back_ref.dtype).reshape(
            last - first, positions, chans
        )
        first = last


def terms_of(pad, scale, flipped, windows_ref, out_ref):
    positions, outs = windows_ref.shape[1], out_ref.shape[2]
    tiles = flipped.shape[1] // positions
    for a in range(3):
        move = pad * (a - 1)
        first, last = max(0, move), min(tiles, tiles + move)
        lhs = flipped[:, first * positions : last * positions]
        rhs = windows_ref[pad + first - move : pad + last - move].reshape(
            (last - first) * positions, 3 * outs
        )
        terms = jnp.dot(lhs, rhs, preferred_element_type=jnp.float32) * scale
        for b in range(3):
            out_ref[3 * a + b] = terms[:, b * outs : (b + 1) * outs]


def other_kernel(pad, scale, me_ref, core_ref, *refs):
    *strip_from, windows_ref, other_ref, mine_ref, strip_ref, flipped_ref, sem = refs
    tiles, positions, chans = strip_ref.shape
    half = chans // 2
    core, me = core_ref[0], me_ref[0]
    stay_ref, got_ref, *pair_refs = strip_from
    places = [(stay_ref.at[pl.ds(0, 1)], 0, 1), (got_ref, 1, 1)]
    places += [(ref, 2 * k, 2) for k, ref in enumerate(pair_refs, 1)]
    wait_all(
        start_all(
            [
                pltpu.make_async_copy(ref, strip_ref.at[pl.ds(first, count)], sem.at[n])
                for n, (ref, first, count) in enumerate(places)
            ]
        )
    )
    for j in range(tiles):
        x = strip_ref[me ^ j]
        low, high = x[:, :half], x[:, half:]
        columns = slice(j * positions, (j + 1) * positions)
        mine_ref[:, columns] = jnp.where(core == 0, low, high).T
        flipped_ref[:, columns] = jnp.where(core == 0, high, low).T
    terms_of(pad, scale, flipped_ref, windows_ref, other_ref)


def mine_kernel(pad, scale, flipped_ref, windows_ref, mine_ref):
    terms_of(pad, scale, flipped_ref, windows_ref, mine_ref)


def join_kernel(half_ref, part_ref, part_x_ref, *refs):
    refs[-1][...] = part_ref[...] + part_x_ref[...]


def vmem(n):
    return [pl.BlockSpec(memory_space=pltpu.VMEM)] * n


def whole(*arrays):
    return [pl.BlockSpec(a.shape, lambda i, n=a.ndim: (0,) * n) for a in arrays]


def quick(inputs, output_gradient, weight):
    rows, width, in_chans = inputs.shape
    outs = output_gradient.shape[2]
    tiles = lax.axis_size("row")
    panel = in_chans // tiles
    positions = rows * width
    shift = DILATION_STEP // rows
    me = lax.axis_index("row").astype(jnp.int32).reshape(1)
    core = (lax.axis_index("col") % 2).astype(jnp.int32).reshape(1)
    params = pltpu.CompilerParams(vmem_limit_bytes=VMEM_LIMIT)
    smem = pl.BlockSpec(memory_space=pltpu.SMEM)

    zs = tiles // 2
    flat = inputs.reshape(positions, in_chans)
    sizes = (zs, 1, 2, 2)
    stay, go_own, go_near, go_far = pl.pallas_call(
        split_kernel,
        grid=(2,),
        out_shape=[jax.ShapeDtypeStruct((n, positions, panel), jnp.bfloat16) for n in sizes],
        in_specs=[
            smem,
            pl.BlockSpec((positions // 2, in_chans), lambda i: (i, 0)),
            pl.BlockSpec((positions // 2, outs), lambda i: (i, 0)),
        ],
        out_specs=[pl.BlockSpec((n, positions // 2, panel), lambda i: (0, i, 0)) for n in sizes],
        compiler_params=params,
        name="split",
    )(me, flat, output_gradient.reshape(positions, outs))
    own = output_gradient.reshape(positions, outs)
    got_far = swap(go_far, "row", 1)
    got = swap(go_near, "row", 1)

    def pack(first, count, arrived):
        return pl.pallas_call(
            lambda *refs: pack_kernel(first, *refs),
            grid=(1,),
            out_shape=[jax.ShapeDtypeStruct((2, positions, panel), jnp.bfloat16)] * count,
            in_specs=whole(stay, arrived),
            out_specs=[pl.BlockSpec((2, positions, panel), lambda i: (0, 0, 0))] * count,
            compiler_params=params,
            name="pack",
        )(stay, arrived)

    far_pairs = pack(2, 2, got_far)
    far = swap(own, "row", 4)
    far, *far_pairs = lax.optimization_barrier((far, *far_pairs))
    rest = jnp.stack([swap(own, "row", 2), far])
    relayed = swap(far, "row", 2)
    pairs = [*pack(1, 1, got), *far_pairs]
    got_own = swap(go_own, "row", 1)
    strip = [stay, got_own] + [swap(p, "row", 2 * k) for k, p in enumerate(pairs, 1)]

    relayed, strip[1] = lax.optimization_barrier((relayed, strip[1]))
    rest_y = swap(rest, "row", 1)
    relayed_y = swap(relayed, "row", 1)
    stacked = jnp.concatenate([own[None], got[1:], rest, relayed[None], rest_y, relayed_y[None]])
    near, beside = rims(stacked.reshape(tiles, rows, width, outs), DILATION_STEP, core)

    pieces = (own, got, rest, rest_y, relayed, relayed_y, near, beside)
    hbm = pl.BlockSpec(memory_space=pltpu.HBM)
    windows = pl.pallas_call(
        windows_kernel,
        out_shape=jax.ShapeDtypeStruct((tiles + 2 * shift, positions, 3 * outs), jnp.bfloat16),
        in_specs=[smem, smem] + [hbm] * 8,
        out_specs=vmem(1)[0],
        scratch_shapes=[
            pltpu.VMEM((tiles, positions, outs), jnp.bfloat16),
            pltpu.VMEM(near.shape, jnp.bfloat16),
            pltpu.VMEM(beside.shape, jnp.bfloat16),
            pltpu.SemaphoreType.DMA((tiles + 2,)),
        ],
        compiler_params=params,
        name="windows",
    )(me, core, *pieces)
    scale = 1.0 / math.sqrt(rows * tiles * width * lax.axis_size("col"))
    half = jax.ShapeDtypeStruct((9, panel // 2, outs), jnp.float32)
    theirs, flipped = pl.pallas_call(
        lambda *refs: other_kernel(shift, scale, *refs),
        out_shape=(half, jax.ShapeDtypeStruct((panel // 2, tiles * positions), jnp.bfloat16)),
        in_specs=[smem, smem] + [hbm] * (zs + 1) + vmem(1),
        out_specs=tuple(vmem(2)),
        scratch_shapes=[
            pltpu.VMEM((tiles, positions, panel), jnp.bfloat16),
            pltpu.VMEM((panel // 2, tiles * positions), jnp.bfloat16),
            pltpu.SemaphoreType.DMA((zs + 1,)),
        ],
        compiler_params=params,
        name="other_terms",
    )(me, core, *strip, windows)
    weight, theirs = lax.optimization_barrier((weight, theirs))
    back = pl.pallas_call(
        lambda *refs: back_kernel(shift, *refs),
        out_shape=jax.ShapeDtypeStruct((tiles, positions, panel), jnp.bfloat16),
        in_specs=vmem(2),
        out_specs=vmem(1)[0],
        scratch_shapes=[pltpu.VMEM((panel, 9 * outs), jnp.bfloat16)],
        compiler_params=params,
        name="back",
    )(windows, weight.reshape(9, panel, outs))
    mine = pl.pallas_call(
        lambda *refs: mine_kernel(shift, scale, *refs),
        out_shape=half,
        in_specs=vmem(2),
        out_specs=vmem(1)[0],
        compiler_params=params,
        name="mine_terms",
    )(flipped, windows)
    chip = mine + swap(theirs, "col", 1)
    chip, back = lax.optimization_barrier((chip, back))
    across = swap(chip, "col", 2)
    other = (swap(chip, "col", 1), swap(across, "col", 1))
    grad_weight = None
    for which, terms in ((core, (chip, across)), (1 - core, other)):
        before = [] if grad_weight is None else [grad_weight]
        block = (9, panel // 2, outs)
        grad_weight = pl.pallas_call(
            join_kernel,
            grid_spec=pltpu.PrefetchScalarGridSpec(
                num_scalar_prefetch=1,
                grid=(1,),
                in_specs=[pl.BlockSpec(block, lambda i, h: (i, 0, 0))] * 2
                + [pl.BlockSpec(memory_space=pl.ANY)] * len(before),
                out_specs=pl.BlockSpec(block, lambda i, h: (i, h[0], 0)),
            ),
            out_shape=jax.ShapeDtypeStruct((9, panel, outs), jnp.float32),
            input_output_aliases={3: 0} if before else {},
            compiler_params=params,
            name="join",
        )(which, *terms, *before)

    grad_back = lax.all_to_all(back, "row", split_axis=0, concat_axis=0, tiled=True)
    grad_back, grad_weight = lax.optimization_barrier((grad_back, grad_weight))
    grad_in = pl.pallas_call(
        merge_kernel,
        grid=(2,),
        out_shape=jax.ShapeDtypeStruct((positions, in_chans), jnp.bfloat16),
        in_specs=[pl.BlockSpec((tiles, positions // 2, panel), lambda i: (0, i, 0))],
        out_specs=pl.BlockSpec((positions // 2, in_chans), lambda i: (i, 0)),
        compiler_params=params,
        name="merge",
    )(grad_back)

    return grad_in.reshape(rows, width, in_chans), grad_weight.reshape(3, 3, panel, outs)


def extended(x, sides, width):
    for axis, dim in sides:
        peers, length = (lax.axis_size(axis), x.shape[dim])
        up = [(i, (i + 1) % peers) for i in range(peers - 1)]
        down = [(j, i) for i, j in up]
        last = lax.slice_in_dim(x, length - width, length, axis=dim)
        initial = lax.slice_in_dim(x, 0, width, axis=dim)
        before = lax.ppermute(last, axis, up)
        after = lax.ppermute(initial, axis, down)
        x = jnp.concatenate([before, x, after], axis=dim)
    return x


def general(inputs, output_gradient, weight):
    height, width, in_chans = inputs.shape
    out_chans = output_gradient.shape[2]
    step = DILATION_STEP
    in_strip = lax.all_to_all(inputs, "row", split_axis=2, concat_axis=0, tiled=True)
    strip_rows = in_strip.shape[0]
    panel = in_strip.shape[2]
    in_padded = jnp.pad(in_strip, ((step, step), (0, 0), (0, 0)))
    side_rimmed = extended(output_gradient, (("col", 1),), step)
    piece = lax.all_gather(side_rimmed, "row", axis=0, tiled=True)
    start = jnp.int32(0)
    grad_padded = jnp.zeros((strip_rows + 2 * step, width, panel), jnp.float32)
    count = piece.shape[0]
    new_terms = []
    for kernel_tap_row in range(3):
        in_rows = lax.dynamic_slice_in_dim(in_padded, step * kernel_tap_row, count, 0).reshape(
            count * width, panel
        )
        back = jnp.zeros((count * width, panel), jnp.float32)
        for kernel_tap_column in range(3):
            left_offset = step * (2 - kernel_tap_column)
            window = piece[:, left_offset : left_offset + width, :].reshape(
                count * width, out_chans
            )
            new_terms.append(
                lax.dot_general(
                    in_rows, window, (((0,), (0,)), ((), ())), preferred_element_type=jnp.float32
                )
            )
            back = back + lax.dot_general(
                window,
                weight[kernel_tap_row, kernel_tap_column],
                (((1,), (1,)), ((), ())),
                preferred_element_type=jnp.float32,
            )
        target = start + step * kernel_tap_row
        current = lax.dynamic_slice_in_dim(grad_padded, target, count, 0)
        grad_padded = lax.dynamic_update_slice_in_dim(
            grad_padded, current + back.reshape(count, width, panel), target, 0
        )
    terms = jnp.stack(new_terms).reshape(3, 3, panel, out_chans)
    terms, grad_padded = (terms, grad_padded)
    grad_strip = grad_padded[step : step + strip_rows].astype(jnp.bfloat16)
    grad_in = lax.all_to_all(grad_strip, "row", split_axis=0, concat_axis=2, tiled=True)
    scale = 1.0 / math.sqrt(height * width * lax.axis_size("row") * lax.axis_size("col"))
    terms = terms * scale
    grad_weight = lax.psum(terms, "col")
    return (grad_in, grad_weight)


def shards(inputs, output_gradient, weight):
    rows, width, in_chans = inputs.shape
    tiles, strips = lax.axis_size("row"), lax.axis_size("col")
    fits = (
        tiles == 8
        and strips == 4
        and DILATION_STEP % rows == 0
        and DILATION_STEP <= width
        and width % 16 == 0
        and in_chans % (tiles * 256) == 0
        and output_gradient.shape[2] % 128 == 0
    )
    return (quick if fits else general)(inputs, output_gradient, weight)


def solution(mesh):
    return jax.shard_map(
        shards,
        mesh=mesh,
        in_specs=(P("row", "col", None), P("row", "col", None), P(None, None, "row", None)),
        out_specs=(P("row", "col", None), P(None, None, "row", None)),
        check_vma=False,
    )
```
